256 devices in a mesh: seq: 64 (over y_hi, z, x), user: 4 (over y_lo, core).
Axes of the slice: x: 4, y: 4 (y_hi: 2, y_lo: 2; y = y_hi * 2 + y_lo), z: 8, core: 2. Of those that a mesh axis runs over, the one named last changes fastest.
Arguments:
- history: bfloat16 [4, 32768, 1024], P('user', 'seq'), may hold values from -6 to 6
- hist_len: int32 [4], P('user'), may hold values from 16384 to 32768, as said below
- cand_start: int32 [4, 16], P('user'), may hold values from 0 to 127
- candidates: bfloat16 [4, 2048, 1024], P('user', 'seq'), may hold values from -6 to 6
- slot_cand: int32 [4, 2048], P('user', 'seq'), may hold values from 0 to 2047, each once within a row
- w_kv: bfloat16 [1024, 2048], P('user'), may hold values from -0.1875 to 0.1875
- w_qu: bfloat16 [1024, 2048], P('user'), may hold values from -0.1875 to 0.1875
- w_o: bfloat16 [1024, 1024], P('user'), may hold values from -0.1875 to 0.1875
Outputs:
- scored: bfloat16 [4, 2048, 1024], P('user', 'seq')
The draws below stay inside these ranges and needn't reach their ends.
Inputs may be any that keep to these rules, and one draw needn't show every extreme that they name: `hist_len`: some user has exactly 32768 positions and another exactly 16384. `slot_cand`: each user's slots hold each of its 2048 candidates once.
All inputs are finite; a program needn't handle non-finite values.
Results may differ from the reference program's by a relative error of at most 0.007.
Values may be sent and summed in bfloat16 or wider, within the bound.
A program may use at most 64 MiB of HBM per device.

```python
import math
import jax
import jax.numpy as jnp
from jax import lax

D = 1024
H = 32
CB = 128
KBLK = 128
HIST = 32768
CAND = 2048
USERS = 4


def draw_hist_len(key, part):
    key = jax.random.fold_in(key, 5)
    first, second = jax.random.split(key)
    base = jax.random.randint(first, (USERS,), HIST // 2, HIST + 1)
    order = jax.random.permutation(second, USERS)
    base = jnp.where(order == 0, HIST, base)
    base = jnp.where(order == 1, HIST // 2, base)
    return base.astype(jnp.int32)


def set_ends(entries, stream_key, smallest, high):
    longest = entries.shape.index(max(entries.shape))
    spots = []
    for shift in (0, 1):
        where = [jax.random.randint(jax.random.fold_in(stream_key, axis), (), 0, length) for axis, length in enumerate(entries.shape)]
        where[longest] = (where[longest] + shift) % entries.shape[longest]
        spots.append(tuple(where))
    return entries.at[spots[0]].set(smallest).at[spots[1]].set(high)


def levels(stream_key, dims, cuts, smallest, high):
    gain, own = 1.0, jax.random.fold_in(stream_key, 6)
    for position, parts in cuts:
        heights = jnp.exp(jax.random.uniform(jax.random.fold_in(own, position), (parts,), jnp.float32, smallest / len(cuts), high / len(cuts)))
        gain = gain * jnp.repeat(heights, dims[position] // parts).reshape([-1 if axis == position else 1 for axis in range(len(dims))])
    return gain


def normal_values(stream_key, dims, scale, bound, pieces=(), kind=jnp.bfloat16):
    array = jax.random.normal(stream_key, dims, jnp.float32) * scale
    if len(pieces) > 0:
        array = levels(stream_key, dims, pieces, -0.22, 0.18) * array
    return jnp.clip(array, min=-bound, max=bound).astype(kind)


def setup_inputs(seed: int = 0) -> dict:
    key_of = jax.random.split(jax.random.key(seed), 9)
    return {
        "history": normal_values(key_of[0], (USERS, HIST, D), 1.0, 6.0, ((0, 4), (1, 64))),
        "hist_len": draw_hist_len(jax.random.fold_in(key_of[8], 71), 0),
        "cand_start": set_ends(jax.random.randint(key_of[2], (USERS, CAND // CB), 0, HIST // (2 * KBLK)), jax.random.fold_in(key_of[2], 1), 0, (HIST // (2 * KBLK)) - 1).astype(jnp.int32),
        "candidates": normal_values(key_of[3], (USERS, CAND, D), 1.0, 6.0, ((0, 4), (1, 64))),
        "slot_cand": jax.vmap(lambda own: jax.random.permutation(own, CAND))(jax.random.split(key_of[4], USERS)).reshape((USERS, CAND)).astype(jnp.int32),
        "w_kv": normal_values(key_of[5], (D, 2 * D), D ** -0.5, 0.1875, ((0, 4),)),
        "w_qu": normal_values(key_of[6], (D, 2 * D), D ** -0.5, 0.1875, ((0, 4),)),
        "w_o": normal_values(key_of[7], (D, D), D ** -0.5, 0.1875, ((0, 4),)),
    }


def layer_norm(rows):
    rows = rows.astype(jnp.float32)
    center = rows - lax.optimization_barrier(jnp.mean(rows, axis=-1, keepdims=True))
    spread = lax.optimization_barrier(jnp.mean(center * center, axis=-1, keepdims=True))
    return center / jnp.sqrt(spread + 1e-05)

def attend(queries, keys, values, visible):
    count = queries.shape[0]
    length = keys.shape[0]
    width = queries.shape[1]
    head_size = width // H
    group = min(8, H)
    groups = H // group
    q_heads = queries.reshape(count, groups, group, head_size).transpose(1, 0, 2, 3)
    k_heads = keys.reshape(length, groups, group, head_size).transpose(1, 0, 2, 3)
    v_heads = values.reshape(length, groups, group, head_size).transpose(1, 0, 2, 3)

    def one_group(items):
        q_part, k_part, v_part = items
        scores = jnp.einsum('rgd,kgd->grk', q_part.astype(jnp.float32), k_part.astype(jnp.float32))
        weights = jnp.where(visible[None], jax.nn.silu(scores), 0.0).astype(jnp.bfloat16)
        return jnp.einsum('grk,kgd->rgd', weights.astype(jnp.float32), v_part.astype(jnp.float32))
    result = lax.map(one_group, (q_heads, k_heads, v_heads))
    return result.transpose(1, 0, 2, 3).reshape(count, width)

def reference(history, hist_len, cand_start, candidates, slot_cand, w_kv, w_qu, w_o):
    width = w_o.shape[0]
    span = math.gcd(512, HIST)

    def one_user(items):
        hist, length, starts, cand, slots = items
        normed_hist = layer_norm(hist).astype(jnp.bfloat16)
        key_value = jax.nn.silu(jnp.dot(normed_hist, w_kv, preferred_element_type=jnp.float32)).astype(jnp.bfloat16)
        keys = key_value[:, :width]
        values = key_value[:, width:]
        normed_cand = layer_norm(cand).astype(jnp.bfloat16)
        query_gate = jax.nn.silu(jnp.dot(normed_cand, w_qu, preferred_element_type=jnp.float32))
        queries = query_gate[:, :width].astype(jnp.bfloat16)
        gates = query_gate[:, width:]
        blocks = (slots // CB)[:, None] == jnp.arange(CAND // CB, dtype=jnp.int32)[None, :]
        lows = lax.optimization_barrier(jnp.sum(jnp.where(blocks, starts[None, :] * KBLK, 0), axis=1)).astype(jnp.int32)

        def step(total, index):
            begin = (index * span).astype(jnp.int32)
            key_rows = lax.dynamic_slice_in_dim(keys, begin, span, 0)
            value_rows = lax.dynamic_slice_in_dim(values, begin, span, 0)
            positions = begin + jnp.arange(span, dtype=jnp.int32)
            visible = (positions[None, :] >= lows[:, None]) & (positions[None, :] < length)
            return (total + attend(queries, key_rows, value_rows, visible), None)
        mixed, unused = lax.scan(step, jnp.zeros((CAND, width), jnp.float32), jnp.arange(HIST // span, dtype=jnp.int32))
        normed_mix = layer_norm(mixed).astype(jnp.bfloat16)
        gated = (lax.optimization_barrier(normed_mix).astype(jnp.float32) * gates).astype(jnp.bfloat16)
        projected = jnp.dot(gated, w_o, preferred_element_type=jnp.float32)
        return (cand.astype(jnp.float32) + projected).astype(jnp.bfloat16)
    return lax.map(one_user, (history, hist_len, cand_start, candidates, slot_cand))
```

```python
import jax
import jax.numpy as jnp
from jax import lax
from jax.experimental import pallas as pl
from jax.experimental.pallas import tpu as pltpu
from jax.sharding import PartitionSpec as P

MESH = pl.DeviceIdType.MESH
F32 = jnp.float32
BF16 = jnp.bfloat16

NX, NY, NZ = 4, 2, 8
SLOTS = 32
OWN = NX * NY
ROWS = OWN * SLOTS
WIDTH = 1024
WIDE = 256
GROUPS = WIDTH // WIDE
HEADS = 8
HEAD = 32
SPAN = 512
KBLK = 128
BLOCKS = SPAN // KBLK
CB = 128
STEPS = 16
QUARTER = 256


def silu(v):
    half = 0.5 * v
    return half + half * jnp.tanh(half)


def normed(rows):
    rows = rows.astype(F32)
    center = rows - jnp.mean(rows, axis=-1, keepdims=True)
    spread = jnp.mean(center * center, axis=-1, keepdims=True)
    return center * lax.rsqrt(spread + 1e-05)


def kernel(
    len_ref, start_ref, slot_ref, hist_ref, cand_ref, wkv_hbm, wqu_hbm, wo_hbm, out_ref,
    wq, wkv, wg, wo, nhist, ncand, gates, keys, vals, qall, masks,
    st1, st2, part, ra, sb, rb, sc, rc, keep, sd, rd,
    w_send, w_recv, w_local, st_send, st1_recv, st2_recv, q_send, q_recv,
    ring_send, ring_recv, a_send, a_recv, b_send, b_recv, c_send, c_recv, d_send, d_recv,
):
    seq = lax.axis_index("seq")
    user = lax.axis_index("user")
    yh = lax.div(seq, NZ * NX)
    z = lax.rem(lax.div(seq, NX), NZ)
    x = lax.rem(seq, NX)
    yl = lax.div(user, 2)
    core = lax.rem(user, 2)
    owner = x * NY + yh

    def seq_of(y_, z_, x_):
        return y_ * (NZ * NX) + z_ * NX + x_

    x_next, x_prev, x_far = lax.rem(x + 1, NX), lax.rem(x + 3, NX), lax.rem(x + 2, NX)
    sib_user = user + 1 - 2 * core
    opp_user = (1 - yl) * 2 + core
    sibling = (seq, sib_user)
    near = (seq, opp_user)
    cross = (seq_of(1 - yh, z, x), opp_user)
    right_x = (seq_of(yh, z, x_next), user)
    left_x = (seq_of(yh, z, x_prev), user)
    mirror = (seq_of(1 - yh, z, x), user)
    up_z = (seq_of(yh, lax.rem(z + 1, NZ), x), user)
    down_z = (seq_of(yh, lax.rem(z + NZ - 1, NZ), x), user)
    flat = []
    for dx in range(NX):
        for dy in range(NY):
            if dx or dy:
                px, py = lax.rem(x + dx, NX), lax.rem(yh + dy, NY)
                flat.append(((seq_of(py, z, px), user), px * NY + py))
    column = []
    for dz in range(1, NZ):
        pz = lax.rem(z + dz, NZ)
        column.append(((seq_of(yh, pz, x), user), pz))

    barrier = pltpu.get_barrier_semaphore()
    peers = [sibling, near, cross] + [p for p, _ in flat] + [p for p, _ in column]
    for peer in peers:
        pl.semaphore_signal(barrier, inc=1, device_id=peer, device_id_type=MESH)
    pl.semaphore_wait(barrier, len(peers))

    def remote(src, dst, send, recv, device):
        return pltpu.make_async_remote_copy(
            src_ref=src, dst_ref=dst, send_sem=send, recv_sem=recv, device_id=device, device_id_type=MESH
        )

    pieces = (
        (wqu_hbm, 0, WIDTH, wq),
        (wkv_hbm, 0, 2 * WIDTH, wkv),
        (wqu_hbm, WIDTH, WIDTH, wg),
        (wo_hbm, 0, WIDTH, wo),
    )

    def own_rows(index):
        return pl.ds(pl.multiple_of(index * QUARTER, QUARTER), QUARTER)

    def w_copy(n, kind):
        hbm, lo, cols, dst = pieces[n]
        half = cols // 2
        if kind == 0:
            return remote(hbm.at[:, pl.ds(lo, cols)], dst.at[own_rows(user), :], w_send.at[n, 0], w_recv.at[n, 0], sibling)
        if kind in (1, 2):
            shift = (kind - 1) * half
            return remote(
                hbm.at[:, pl.ds(lo + shift, half)], dst.at[own_rows(user), pl.ds(shift, half)],
                w_send.at[n, kind], w_recv.at[n, kind], near if kind == 1 else cross,
            )
        shift = (kind - 3) * half
        ref = dst.at[own_rows(opp_user), pl.ds(shift, half)]
        return remote(ref, ref, w_send.at[n, kind], w_recv.at[n, kind], sibling)

    def w_mine(n):
        hbm, lo, cols, dst = pieces[n]
        return pltpu.make_async_copy(hbm.at[:, pl.ds(lo, cols)], dst.at[own_rows(user), :], w_local.at[n])

    def w_start(n):
        for kind in (1, 2, 0):
            w_copy(n, kind).start()
        w_mine(n).start()

    def w_arrived(n, kind):
        _, _, cols, dst = pieces[n]
        half = cols // 2
        if kind == 0:
            ref = dst.at[own_rows(sib_user), :]
        elif kind in (1, 2):
            ref = dst.at[own_rows(opp_user), pl.ds((kind - 1) * half, half)]
        else:
            ref = dst.at[own_rows((1 - yl) * 2 + 1 - core), pl.ds((kind - 3) * half, half)]
        remote(ref, ref, w_send.at[n, kind], w_recv.at[n, kind], sibling).wait_recv()

    def w_forward(n):
        for kind in (1, 2):
            w_arrived(n, kind)
            w_copy(n, kind + 2).start()

    def w_finish(n):
        w_mine(n).wait()
        w_arrived(n, 0)
        w_arrived(n, 3)
        w_arrived(n, 4)

    def w_sent(n, kinds):
        for kind in kinds:
            w_copy(n, kind).wait_send()

    w_start(0)

    slots = slot_ref[...]
    window = jnp.zeros(slots.shape, F32)
    for c in range(start_ref.shape[1]):
        begin = start_ref[0, c].astype(F32)
        window = window + jnp.where((slots >= c * CB) & (slots < (c + 1) * CB), begin, 0.0)
    st1[owner] = jnp.zeros((8, 128), F32)
    st1[owner, 0:1, 0:SLOTS] = window
    for n, (peer, _) in enumerate(flat):
        remote(st1.at[owner], st1.at[owner], st_send.at[0, n], st1_recv.at[owner], peer).start()

    ncand[...] = normed(cand_ref[...]).astype(BF16)

    def clear(n, carry):
        keys[lax.div(n, BLOCKS), lax.rem(n, BLOCKS)] = jnp.zeros((WIDE, HEADS * KBLK), BF16)
        vals[lax.div(n, BLOCKS), lax.rem(n, BLOCKS)] = jnp.zeros((HEADS * KBLK, WIDE), BF16)
        return carry

    lax.fori_loop(0, GROUPS * BLOCKS, clear, 0)

    for n, (peer, o) in enumerate(flat):
        remote(st1.at[o], st1.at[o], st_send.at[0, n], st1_recv.at[o], peer).wait_recv()
    st2[z] = jnp.concatenate([st1[o, 0:1, :] for o in range(OWN)], axis=0)
    for n, (peer, _) in enumerate(column):
        remote(st2.at[z], st2.at[z], st_send.at[1, n], st2_recv.at[z], peer).start()

    w_sent(0, (1, 2))
    w_start(1)
    w_forward(0)
    w_finish(0)

    queries = silu(jnp.dot(ncand[...], wq[...], preferred_element_type=F32)).astype(BF16)
    mine = pl.ds(pl.multiple_of(owner * SLOTS, SLOTS), SLOTS)
    for g in range(GROUPS):
        qall[z, g, mine, :] = queries[:, g * WIDE:(g + 1) * WIDE]
    for n, (peer, _) in enumerate(flat):
        ref = qall.at[z, :, mine, :]
        remote(ref, ref, q_send.at[n], q_recv.at[owner], peer).start()

    def norm_rows(n, carry):
        rows = pl.ds(pl.multiple_of(n * 64, 64), 64)
        nhist[rows, :] = normed(hist_ref[rows, :]).astype(BF16)
        return carry

    lax.fori_loop(0, SPAN // 64, norm_rows, 0)

    for n, (peer, pz) in enumerate(column):
        remote(st2.at[pz], st2.at[pz], st_send.at[1, n], st2_recv.at[pz], peer).wait_recv()
    lane = lax.broadcasted_iota(jnp.int32, (SLOTS, 128), 1)
    line = lax.broadcasted_iota(jnp.int32, (SLOTS, 128), 0)
    first = (seq * BLOCKS).astype(F32)

    def make_masks(n, carry):
        tile = st2[n]
        for o in range(OWN):
            spread = jnp.broadcast_to(tile[o:o + 1, :], (SLOTS, 128))
            begin = jnp.sum(jnp.where(lane == line, spread, 0.0), axis=1, keepdims=True)
            begin = jnp.broadcast_to(begin, (SLOTS, 128))
            for j in range(BLOCKS):
                masks[n, j, o * SLOTS:(o + 1) * SLOTS, :] = jnp.where(begin <= first + j, 1.0, 0.0).astype(BF16)
        return carry

    lax.fori_loop(0, NZ, make_masks, 0)

    for n, (peer, o) in enumerate(flat):
        ref = qall.at[z, :, pl.ds(pl.multiple_of(o * SLOTS, SLOTS), SLOTS), :]
        remote(ref, ref, q_send.at[n], q_recv.at[o], peer).wait_recv()

    def ring(side, index, z_of, g):
        ref = qall.at[z_of, g]
        return remote(ref, ref, ring_send.at[side, index], ring_recv.at[side, index], up_z if side == 0 else down_z)

    for g in range(GROUPS):
        ring(0, g, z, g).start()
        ring(1, g, z, g).start()

    w_sent(1, (1, 2))
    w_start(2)
    w_forward(1)
    w_finish(1)

    place = lax.broadcasted_iota(jnp.int32, (SPAN, WIDE), 0) + seq * SPAN
    exists = jnp.where(place < len_ref[0], 0.5, 0.0)
    spot = lax.broadcasted_iota(jnp.int32, (KBLK, 128), 1)
    for g in range(GROUPS):
        k = silu(jnp.dot(nhist[...], wkv[:, g * WIDE:(g + 1) * WIDE], preferred_element_type=F32))
        k = k.astype(BF16).astype(F32) * exists
        kt = k.T.astype(BF16)
        for j in range(BLOCKS):
            for h in range(HEADS):
                keys[g, j, h * HEAD:(h + 1) * HEAD, h * KBLK:(h + 1) * KBLK] = (
                    kt[h * HEAD:(h + 1) * HEAD, j * KBLK:(j + 1) * KBLK]
                )
        v = silu(jnp.dot(nhist[...], wkv[:, WIDTH + g * WIDE:WIDTH + (g + 1) * WIDE], preferred_element_type=F32))
        for j in range(BLOCKS):
            for h in range(HEADS):
                side, at = (h * HEAD) // 128 * 128, (h * HEAD) % 128
                own = v[j * KBLK:(j + 1) * KBLK, side:side + 128]
                own = jnp.where((spot >= at) & (spot < at + HEAD), own, 0.0).astype(BF16)
                vals[g, j, h * KBLK:(h + 1) * KBLK, side:side + 128] = own

    def piece(it, side):
        ahead = lax.div(STEPS - 1 - it, STEPS - 1)
        last = lax.div(it, STEPS - 1)
        mid = 1 - ahead - last
        k = it - 1 + ahead - last
        hop = mid * (1 + lax.div(k, GROUPS))
        if side == 0:
            return lax.rem(z + NZ - hop, NZ), mid * lax.rem(k, GROUPS) + 2 * last
        return lax.rem(z + hop, NZ), mid * (lax.rem(k, GROUPS) + 2 * lax.div(k, 12)) + ahead + 3 * last

    def attend(z_of, g, p):
        total = jnp.zeros((ROWS, WIDE), F32)
        for j in range(BLOCKS):
            mask = masks[z_of, j]
            q = qall[z_of, g] * jnp.concatenate([mask, mask], axis=1)
            for i in range(4):
                cols = slice(i * WIDE, (i + 1) * WIDE)
                s = jnp.dot(q, keys[g, j, :, cols], preferred_element_type=F32)
                w = (s + s * jnp.tanh(s)).astype(BF16)
                total = total + jnp.dot(w, vals[g, j, cols, :], preferred_element_type=F32)
        part[p] = total.astype(BF16)

    def x_rows(x_of):
        return pl.ds(pl.multiple_of(x_of * (NY * SLOTS), NY * SLOTS), NY * SLOTS)

    def a_copy(p, side):
        lanes = pl.ds(side * 128, 128)
        return remote(
            part.at[p, x_rows(x_far), lanes], ra.at[side, p], a_send.at[side, p], a_recv.at[side, p],
            right_x if side == 0 else left_x,
        )

    def b_copy(p, side):
        return remote(
            sb.at[side, p], rb.at[side, p], b_send.at[side, p], b_recv.at[side, p], right_x if side == 0 else left_x
        )

    def c_copy(p):
        return remote(sc.at[p], rc.at[p], c_send.at[p], c_recv.at[p], mirror)

    def d_copy(p, z_of, g):
        return remote(sd.at[p], rd.at[z, g], d_send.at[p], d_recv.at[z, g], (seq_of(yh, z_of, x), user))

    def stage_b(it):
        for s in range(2):
            p = 2 * it + s
            for side in range(2):
                a_copy(p, side).wait()
                toward = x_next if side == 0 else x_prev
                sb[side, p] = part[p, x_rows(toward), :]
                lanes = slice(side * 128, side * 128 + 128)
                own = part[p, x_rows(toward), lanes].astype(F32) + ra[side, p].astype(F32)
                sb[side, p, :, lanes] = own.astype(BF16)
                b_copy(p, side).start()

    def stage_c(it):
        for s in range(2):
            p = 2 * it + s
            b_copy(p, 0).wait()
            b_copy(p, 1).wait()

            def some(y_of):
                rows = pl.ds(pl.multiple_of(y_of * SLOTS, SLOTS), SLOTS)
                at = pl.ds(pl.multiple_of(x * (NY * SLOTS) + y_of * SLOTS, SLOTS), SLOTS)
                return part[p, at, :].astype(F32) + rb[0, p, rows, :].astype(F32) + rb[1, p, rows, :].astype(F32)

            sc[p] = some(1 - yh).astype(BF16)
            c_copy(p).start()
            keep[p] = some(yh)

    def stage_d(it, own):
        for s in range(2):
            p = 2 * it + s
            c_copy(p).wait()
            total = keep[p] + rc[p].astype(F32)
            z_of, g = piece(it, s)
            if own:
                rd[z, g] = total.astype(BF16)
            else:
                sd[p] = total.astype(BF16)
                d_copy(p, z_of, g).start()

    def step(it, carry):
        k = it - 1

        @pl.when((it >= 1) & (it < STEPS - 1))
        def _():
            for side in range(2):
                z_of, g = piece(it, side)
                ring(side, k, z_of, g).wait_recv()

        @pl.when((it >= 1) & (k < 10))
        def _():
            z_of, g = piece(it, 0)
            ring(0, k + 4, z_of, g).start()

        @pl.when((it >= 1) & (k < 8))
        def _():
            z_of, g = piece(it, 1)
            ring(1, k + 4, z_of, g).start()

        @pl.when((k == 10) | (k == 11))
        def _():
            z_of, g = piece(it, 1)
            ring(1, k + 2, z_of, g).start()

        @pl.when(it >= 2)
        def _():
            stage_b(it - 2)

        @pl.when(it >= 3)
        def _():
            stage_c(it - 3)

        @pl.when(it == 4)
        def _():
            stage_d(0, True)

        @pl.when(it >= 5)
        def _():
            stage_d(it - 4, False)

        @pl.when(it == 4)
        def _():
            w_sent(2, (1, 2))
            w_start(3)
            w_forward(2)

        @pl.when(it == 8)
        def _():
            w_forward(3)

        for side in range(2):
            z_of, g = piece(it, side)
            attend(z_of, g, 2 * it + side)
            a_copy(2 * it + side, 0).start()
            a_copy(2 * it + side, 1).start()
        return carry

    lax.fori_loop(0, STEPS, step, 0)

    stage_b(STEPS - 2)
    stage_c(STEPS - 3)
    stage_d(STEPS - 4, False)
    w_finish(2)
    w_finish(3)
    gates[...] = silu(jnp.dot(ncand[...], wg[...], preferred_element_type=F32))
    stage_b(STEPS - 1)
    stage_c(STEPS - 2)
    stage_d(STEPS - 3, False)
    stage_c(STEPS - 1)
    stage_d(STEPS - 2, False)
    stage_d(STEPS - 1, True)

    for _, pz in column:
        for g in range(GROUPS):
            remote(sd.at[0], rd.at[pz, g], d_send.at[0], d_recv.at[pz, g], sibling).wait_recv()
    mixed = jnp.concatenate(
        [sum(rd[n, g].astype(F32) for n in range(NZ)) for g in range(GROUPS)], axis=1
    )
    gated = (normed(mixed).astype(BF16).astype(F32) * gates[...]).astype(BF16)
    projected = jnp.dot(gated, wo[...], preferred_element_type=F32)
    out_ref[...] = (cand_ref[...].astype(F32) + projected).astype(BF16)

    w_sent(0, (0, 3, 4))
    w_sent(1, (0, 3, 4))
    w_sent(2, (0, 3, 4))
    w_sent(3, (0, 1, 2, 3, 4))
    for n, (peer, _) in enumerate(flat):
        remote(st1.at[owner], st1.at[owner], st_send.at[0, n], st1_recv.at[owner], peer).wait_send()
        ref = qall.at[z, :, mine, :]
        remote(ref, ref, q_send.at[n], q_recv.at[owner], peer).wait_send()
    for n, (peer, _) in enumerate(column):
        remote(st2.at[z], st2.at[z], st_send.at[1, n], st2_recv.at[z], peer).wait_send()

    def ring_sent(n, carry):
        for side in range(2):
            ring(side, n, z, 0).wait_send()
        return carry

    lax.fori_loop(0, 14, ring_sent, 0)

    def d_sent(n, carry):
        remote(sd.at[n], rd.at[z, 0], d_send.at[n], d_recv.at[z, 0], sibling).wait_send()
        return carry

    lax.fori_loop(2, 2 * STEPS - 2, d_sent, 0)


def local(history, hist_len, cand_start, candidates, slot_cand, w_kv, w_qu, w_o):
    pieces = 2 * STEPS
    vmem = pl.BlockSpec(memory_space=pltpu.VMEM)
    smem = pl.BlockSpec(memory_space=pltpu.SMEM)
    anywhere = pl.BlockSpec(memory_space=pl.ANY)
    dma = pltpu.SemaphoreType.DMA
    out = pl.pallas_call(
        kernel,
        out_shape=jax.ShapeDtypeStruct((SLOTS, WIDTH), BF16),
        in_specs=[smem, smem, vmem, vmem, vmem, anywhere, anywhere, anywhere],
        out_specs=vmem,
        scratch_shapes=[
            pltpu.VMEM((WIDTH, WIDTH), BF16),
            pltpu.VMEM((WIDTH, 2 * WIDTH), BF16),
            pltpu.VMEM((WIDTH, WIDTH), BF16),
            pltpu.VMEM((WIDTH, WIDTH), BF16),
            pltpu.VMEM((SPAN, WIDTH), BF16),
            pltpu.VMEM((SLOTS, WIDTH), BF16),
            pltpu.VMEM((SLOTS, WIDTH), F32),
            pltpu.VMEM((GROUPS, BLOCKS, WIDE, HEADS * KBLK), BF16),
            pltpu.VMEM((GROUPS, BLOCKS, HEADS * KBLK, WIDE), BF16),
            pltpu.VMEM((NZ, GROUPS, ROWS, WIDE), BF16),
            pltpu.VMEM((NZ, BLOCKS, ROWS, 128), BF16),
            pltpu.VMEM((OWN, 8, 128), F32),
            pltpu.VMEM((NZ, 8, 128), F32),
            pltpu.VMEM((pieces, ROWS, WIDE), BF16),
            pltpu.VMEM((2, pieces, NY * SLOTS, 128), BF16),
            pltpu.VMEM((2, pieces, NY * SLOTS, WIDE), BF16),
            pltpu.VMEM((2, pieces, NY * SLOTS, WIDE), BF16),
            pltpu.VMEM((pieces, SLOTS, WIDE), BF16),
            pltpu.VMEM((pieces, SLOTS, WIDE), BF16),
            pltpu.VMEM((pieces, SLOTS, WIDE), F32),
            pltpu.VMEM((pieces, SLOTS, WIDE), BF16),
            pltpu.VMEM((NZ, GROUPS, SLOTS, WIDE), BF16),
            dma((4, 5)), dma((4, 5)), dma((4,)),
            dma((2, 7)), dma((OWN,)), dma((NZ,)),
            dma((7,)), dma((OWN,)),
            dma((2, 14)), dma((2, 14)),
            dma((2, pieces)), dma((2, pieces)),
            dma((2, pieces)), dma((2, pieces)),
            dma((pieces,)), dma((pieces,)),
            dma((pieces,)), dma((NZ, GROUPS)),
        ],
        compiler_params=pltpu.CompilerParams(
            collective_id=0, has_side_effects=True, vmem_limit_bytes=60 * 2**20
        ),
    )(hist_len, cand_start, slot_cand, history[0], candidates[0], w_kv, w_qu, w_o)
    return out[None]


def solution(mesh):
    in_specs = (
        P("user", "seq", None),
        P("user"),
        P("user", None),
        P("user", "seq", None),
        P("user", "seq"),
        P("user", None),
        P("user", None),
        P("user", None),
    )
    out_specs = P("user", "seq", None)
    return jax.shard_map(local, mesh=mesh, in_specs=in_specs, out_specs=out_specs, check_vma=False)
```

```python
import jax
import jax.numpy as jnp
from jax import lax
from jax.experimental import pallas as pl
from jax.experimental.pallas import tpu as pltpu
from jax.sharding import PartitionSpec as P

MESH = pl.DeviceIdType.MESH
F32 = jnp.float32
BF16 = jnp.bfloat16

NX, NY, NZ = 4, 2, 8
SLOTS = 32
OWN = NX * NY
ROWS = OWN * SLOTS
WIDTH = 1024
WIDE = 256
GROUPS = WIDTH // WIDE
HEADS = 8
HEAD = 32
SPAN = 512
KBLK = 128
BLOCKS = SPAN // KBLK
CB = 128
STEPS = 16
CUT = 12
LAG = 4
QUARTER = 256


def silu(v):
    half = 0.5 * v
    return half + half * jnp.tanh(half)


def normed(rows):
    rows = rows.astype(F32)
    center = rows - jnp.mean(rows, axis=-1, keepdims=True)
    spread = jnp.mean(center * center, axis=-1, keepdims=True)
    return center * lax.rsqrt(spread + 1e-05)


def kernel(
    len_ref, start_ref, slot_ref, hist_ref, cand_ref, wkv_hbm, wqu_hbm, wo_hbm, out_ref,
    wqu, wkv, wo, nhist, ncand, cin, pq, pg, rq, rg, keys, vals, qall, masks,
    st1, st2, part, dr, sc, keep, sd, rd, rown,
    w_send, w_recv, w_local, p_send, p_recv, p_local, st_send, st1_recv, st2_recv, q_send, q_recv,
    ring_send, ring_recv, x_send, x_recv, y_send, y_recv, d_send, d_recv,
):
    seq = lax.axis_index("seq")
    user = lax.axis_index("user")
    yh = lax.div(seq, NZ * NX)
    z = lax.rem(lax.div(seq, NX), NZ)
    x = lax.rem(seq, NX)
    yl = lax.div(user, 2)
    core = lax.rem(user, 2)
    owner = x * NY + yh

    def seq_of(y_, z_, x_):
        return y_ * (NZ * NX) + z_ * NX + x_

    sib_user = user + 1 - 2 * core
    opp_user = (1 - yl) * 2 + core
    sibling = (seq, sib_user)
    near = (seq, opp_user)
    cross = (seq_of(1 - yh, z, x), opp_user)
    mirror = (seq_of(1 - yh, z, x), user)
    opposite = [(s_, (1 - yl) * 2 + k) for s_ in (seq, seq_of(1 - yh, z, x)) for k in range(2)]
    up_z = (seq_of(yh, lax.rem(z + 1, NZ), x), user)
    down_z = (seq_of(yh, lax.rem(z + NZ - 1, NZ), x), user)
    row = []
    for dx in range(1, NX):
        px = lax.rem(x + dx, NX)
        row.append(((seq_of(yh, z, px), user), px))
    flat = []
    for dx in range(NX):
        for dy in range(NY):
            if dx or dy:
                px, py = lax.rem(x + dx, NX), lax.rem(yh + dy, NY)
                flat.append(((seq_of(py, z, px), user), px * NY + py))
    column = []
    for dz in range(1, NZ):
        pz = lax.rem(z + dz, NZ)
        column.append(((seq_of(yh, pz, x), user), pz))

    barrier = pltpu.get_barrier_semaphore()
    peers = [sibling] + opposite + [p for p, _ in flat] + [p for p, _ in column]
    for peer in peers:
        pl.semaphore_signal(barrier, inc=1, device_id=peer, device_id_type=MESH)

    slots = slot_ref[...]
    window = jnp.zeros(slots.shape, F32)
    for c in range(start_ref.shape[1]):
        begin = start_ref[0, c].astype(F32)
        window = window + jnp.where((slots >= c * CB) & (slots < (c + 1) * CB), begin, 0.0)
    st1[owner] = jnp.zeros((8, 128), F32)
    st1[owner, 0:1, 0:SLOTS] = window
    pltpu.make_async_copy(wqu_hbm, wqu, p_local).start()
    rows = normed(cand_ref[...]).astype(BF16)
    for u in range(4):
        ncand[u] = rows[:, u * QUARTER:(u + 1) * QUARTER]
    cin[0:SLOTS, :] = ncand[user]

    def clear(n, carry):
        keys[lax.div(n, BLOCKS), lax.rem(n, BLOCKS)] = jnp.zeros((WIDE, HEADS * KBLK), BF16)
        vals[lax.div(n, BLOCKS), lax.rem(n, BLOCKS)] = jnp.zeros((HEADS * KBLK, WIDE), BF16)
        return carry

    lax.fori_loop(0, GROUPS * BLOCKS, clear, 0)
    pl.semaphore_wait(barrier, len(peers))

    def remote(src, dst, send, recv, device):
        return pltpu.make_async_remote_copy(
            src_ref=src, dst_ref=dst, send_sem=send, recv_sem=recv, device_id=device, device_id_type=MESH
        )

    def halves(hbm, lo, cols, dst):
        return tuple((hbm, lo + s * (cols // 2), dst, s * (cols // 2), cols // 2) for s in range(2))

    pieces = []
    for g in range(GROUPS):
        pieces.append(tuple((wkv_hbm, s * WIDTH + g * WIDE, wkv, s * WIDTH + g * WIDE, WIDE) for s in range(2)))
    pieces += [halves(wo_hbm, 0, WIDTH, wo)]
    W_OUT = GROUPS

    def own_rows(index):
        return pl.ds(pl.multiple_of(index * QUARTER, QUARTER), QUARTER)

    def w_copy(n, kind):
        hbm, lo, dst, at, cols = pieces[n][kind % 2]
        sems = (w_send.at[n, kind], w_recv.at[n, kind])
        if kind < 4:
            target = (near, cross, sibling, sibling)[kind]
            return remote(hbm.at[:, pl.ds(lo, cols)], dst.at[own_rows(user), pl.ds(at, cols)], *sems, target)
        ref = dst.at[own_rows(opp_user), pl.ds(at, cols)]
        return remote(ref, ref, *sems, sibling)

    def w_mine(n, s):
        hbm, lo, dst, at, cols = pieces[n][s]
        return pltpu.make_async_copy(hbm.at[:, pl.ds(lo, cols)], dst.at[own_rows(user), pl.ds(at, cols)], w_local.at[n, s])

    def w_start(n):
        for kind in range(4):
            w_copy(n, kind).start()
        for s in range(2):
            w_mine(n, s).start()

    def w_arrived(n, kind):
        _, _, dst, at, cols = pieces[n][kind % 2]
        rows = (opp_user, sib_user, (1 - yl) * 2 + 1 - core)[kind // 2]
        ref = dst.at[own_rows(rows), pl.ds(at, cols)]
        remote(ref, ref, w_send.at[n, kind], w_recv.at[n, kind], sibling).wait_recv()

    def w_forward(n):
        for kind in (0, 1):
            w_arrived(n, kind)
            w_copy(n, kind + 4).start()

    def w_finish(n):
        for s in range(2):
            w_mine(n, s).wait()
        for kind in range(2, 6):
            w_arrived(n, kind)

    def w_sent(n, kinds):
        for kind in kinds:
            w_copy(n, kind).wait_send()

    half = SLOTS // 2
    near_at = pl.ds(pl.multiple_of(2 * SLOTS + half * core, half), half)
    cross_at = pl.ds(pl.multiple_of(3 * SLOTS + half * core, half), half)

    def in_copy(n):
        if n == 0:
            return remote(ncand.at[sib_user], cin.at[pl.ds(SLOTS, SLOTS), :], p_send.at[0, 0], p_recv.at[0, 0], sibling)
        far, k = divmod(n - 1, 2)
        return remote(
            ncand.at[(1 - yl) * 2 + k, pl.ds(far * half, half), :], cin.at[cross_at if far else near_at, :],
            p_send.at[0, n], p_recv.at[0, 1 + 2 * far + core], opposite[n - 1],
        )

    def in_arrived(n):
        size = SLOTS if n == 0 else half
        ref = cin.at[pl.ds(0 if n == 0 else 2 * SLOTS, size), :]
        remote(ref, ref, p_send.at[0, n], p_recv.at[0, n], sibling).wait_recv()

    def back_copy(m, n):
        src, dst = ((pq, rq), (pg, rg))[m - 1]
        if n == 0:
            return remote(src.at[pl.ds(SLOTS, SLOTS), :], dst.at[0], p_send.at[m, 0], p_recv.at[m, 0], sibling)
        far, k = divmod(n - 1, 2)
        return remote(
            src.at[pl.ds((2 + far) * SLOTS + k * half, half), :], dst.at[1 + core, pl.ds(far * half, half), :],
            p_send.at[m, n], p_recv.at[m, 1 + 2 * far + core], opposite[n - 1],
        )

    def back_arrived(m, n):
        dst = (rq, rg)[m - 1]
        ref = dst.at[0] if n == 0 else dst.at[1, pl.ds(0, half), :]
        remote(ref, ref, p_send.at[m, n], p_recv.at[m, n], sibling).wait_recv()

    for n in range(5):
        in_copy(n).start()
    w_start(0)
    w_start(1)
    for n, (peer, _) in enumerate(flat):
        remote(st1.at[owner], st1.at[owner], st_send.at[0, n], st1_recv.at[owner], peer).start()

    pltpu.make_async_copy(wqu_hbm, wqu, p_local).wait()
    for n in range(5):
        in_arrived(n)
    pq[...] = jnp.dot(cin[...], wqu[:, :WIDTH], preferred_element_type=F32)
    for n in range(5):
        back_copy(1, n).start()

    def norm_rows(n, carry):
        rows = pl.ds(pl.multiple_of(n * 64, 64), 64)
        nhist[rows, :] = normed(hist_ref[rows, :]).astype(BF16)
        return carry

    lax.fori_loop(0, SPAN // 64, norm_rows, 0)

    for n, (peer, o) in enumerate(flat):
        remote(st1.at[o], st1.at[o], st_send.at[0, n], st1_recv.at[o], peer).wait_recv()
    st2[z] = jnp.concatenate([st1[o, 0:1, :] for o in range(OWN)], axis=0)
    for n, (peer, _) in enumerate(column):
        remote(st2.at[z], st2.at[z], st_send.at[1, n], st2_recv.at[z], peer).start()

    w_sent(0, (0, 1))
    w_start(2)

    for n in range(5):
        back_arrived(1, n)
    queries = silu(pq[0:SLOTS, :] + rq[0] + rq[1] + rq[2]).astype(BF16)
    mine = pl.ds(pl.multiple_of(owner * SLOTS, SLOTS), SLOTS)

    def q_copy(g, n):
        ref = qall.at[z, g, mine, :]
        return remote(ref, ref, q_send.at[g], q_recv.at[g], flat[n][0])

    others = pl.ds(0, (OWN - 1) * SLOTS)

    def q_all(g):
        ref = qall.at[z, g, others, :]
        return remote(ref, ref, q_send.at[g], q_recv.at[g], mirror)

    for g in range(GROUPS):
        qall[z, g, mine, :] = queries[:, g * WIDE:(g + 1) * WIDE]
    for g in range(2):
        for n in range(OWN - 1):
            q_copy(g, n).start()

    def ring(side, index, z_of, g):
        ref = qall.at[z_of, g]
        return remote(ref, ref, ring_send.at[side, index], ring_recv.at[side, index], up_z if side == 0 else down_z)

    def ring_begin(g):
        q_all(g).wait_recv()
        ring(0, g, z, g).start()
        ring(1, g, z, g).start()

    def project(g):
        place = lax.broadcasted_iota(jnp.int32, (SPAN, WIDE), 0) + seq * SPAN
        exists = jnp.where(place < len_ref[0], 0.5, 0.0)
        spot = lax.broadcasted_iota(jnp.int32, (KBLK, 128), 1)
        k = silu(jnp.dot(nhist[...], wkv[:, g * WIDE:(g + 1) * WIDE], preferred_element_type=F32))
        k = k.astype(BF16).astype(F32) * exists
        kt = k.T.astype(BF16)
        for j in range(BLOCKS):
            for h in range(HEADS):
                keys[g, j, h * HEAD:(h + 1) * HEAD, h * KBLK:(h + 1) * KBLK] = (
                    kt[h * HEAD:(h + 1) * HEAD, j * KBLK:(j + 1) * KBLK]
                )
        v = silu(jnp.dot(nhist[...], wkv[:, WIDTH + g * WIDE:WIDTH + (g + 1) * WIDE], preferred_element_type=F32))
        for j in range(BLOCKS):
            for h in range(HEADS):
                side, at = (h * HEAD) // 128 * 128, (h * HEAD) % 128
                own = v[j * KBLK:(j + 1) * KBLK, side:side + 128]
                own = jnp.where((spot >= at) & (spot < at + HEAD), own, 0.0).astype(BF16)
                vals[g, j, h * KBLK:(h + 1) * KBLK, side:side + 128] = own

    w_forward(0)
    w_sent(1, (0, 1))
    w_start(3)
    w_forward(1)
    for g in range(2, GROUPS):
        for n in range(OWN - 1):
            q_copy(g, n).start()
    pg[...] = jnp.dot(cin[...], wqu[:, WIDTH:], preferred_element_type=F32)
    w_finish(0)
    project(0)
    for n, (peer, pz) in enumerate(column):
        remote(st2.at[pz], st2.at[pz], st_send.at[1, n], st2_recv.at[pz], peer).wait_recv()
    lane = lax.broadcasted_iota(jnp.int32, (SLOTS, 128), 1)
    line = lax.broadcasted_iota(jnp.int32, (SLOTS, 128), 0)
    first = (seq * BLOCKS).astype(F32)

    def make_masks(n, carry):
        tile = st2[n]
        for o in range(OWN):
            spread = jnp.broadcast_to(tile[o:o + 1, :], (SLOTS, 128))
            begin = jnp.sum(jnp.where(lane == line, spread, 0.0), axis=1, keepdims=True)
            begin = jnp.broadcast_to(begin, (SLOTS, 128))
            for j in range(BLOCKS):
                masks[n, j, o * SLOTS:(o + 1) * SLOTS, :] = jnp.where(begin <= first + j, 1.0, 0.0).astype(BF16)
        return carry

    lax.fori_loop(0, NZ, make_masks, 0)

    w_finish(1)
    project(1)
    ring_begin(0)
    ring_begin(1)

    def piece(it, side):
        ahead = lax.div(STEPS - 1 - it, STEPS - 1)
        last = lax.div(it, STEPS - 1)
        mid = 1 - ahead - last
        k = it - 1 + ahead - last
        hop = mid * (1 + lax.div(k, GROUPS))
        if side == 0:
            return lax.rem(z + NZ - hop, NZ), mid * lax.rem(k, GROUPS) + 2 * last
        return lax.rem(z + hop, NZ), mid * (lax.rem(k, GROUPS) + 2 * lax.div(k, 12)) + ahead + 3 * last

    def attend(z_of, g, p):
        total = jnp.zeros((ROWS, WIDE), F32)
        for j in range(BLOCKS):
            mask = masks[z_of, j]
            q = qall[z_of, g] * jnp.concatenate([mask, mask], axis=1)
            for i in range(4):
                cols = slice(i * WIDE, (i + 1) * WIDE)
                s = jnp.dot(q, keys[g, j, :, cols], preferred_element_type=F32)
                w = (s + s * jnp.tanh(s)).astype(BF16)
                total = total + jnp.dot(w, vals[g, j, cols, :], preferred_element_type=F32)
        part[p] = total.astype(BF16)

    def owner_rows(o):
        return pl.ds(pl.multiple_of(o * SLOTS, SLOTS), SLOTS)

    def places(n, count):
        return pl.ds(n * SLOTS, count * SLOTS)

    def first_copies(p, s):
        if s == 0:
            for n, (peer, px) in enumerate(row):
                rows = pl.ds(pl.multiple_of(px * (NY * SLOTS), NY * SLOTS), NY * SLOTS)
                remote(part.at[p, rows, :], dr.at[p, places(2 * n, 2), :], x_send.at[p], x_recv.at[p], peer).start()
        else:
            for n in range(NX):
                rows = owner_rows(n * NY + 1 - yh)
                remote(part.at[p, rows, :], dr.at[p, places(n, 1), :], x_send.at[p], x_recv.at[p], mirror).start()

    def first_all(p, s):
        ref = dr.at[p, places(0, (6, 4)[s]), :]
        return remote(ref, ref, x_send.at[p], x_recv.at[p], mirror)

    def second_copies(p, s):
        if s == 0:
            src = sc.at[p, places(0, 1), :]
            remote(src, dr.at[p, places(6, 1), :], y_send.at[p], y_recv.at[p], mirror).start()
        else:
            for n, (peer, _) in enumerate(row):
                src = sc.at[p, places(n, 1), :]
                remote(src, dr.at[p, places(4 + n, 1), :], y_send.at[p], y_recv.at[p], peer).start()

    def second_all(p, s):
        ref = dr.at[p, places(6, 1) if s == 0 else places(4, 3), :]
        return remote(ref, ref, y_send.at[p], y_recv.at[p], mirror)

    def o_copy(p, n):
        peer, o = flat[n]
        return remote(part.at[p, owner_rows(o), :], dr.at[p, pl.ds(n * SLOTS, SLOTS), :], x_send.at[p], x_recv.at[p], peer)

    def o_all(p):
        ref = dr.at[p]
        return remote(ref, ref, x_send.at[p], x_recv.at[p], mirror)

    def d_copy(p, z_of, g):
        hop = lax.rem(z + NZ - z_of, NZ) - 1
        return remote(sd.at[p], rd.at[hop, g], d_send.at[p], d_recv, (seq_of(yh, z_of, x), user))

    def deliver(it, s, total, own):
        p = 2 * it + s
        z_of, g = piece(it, s)
        if own:
            rown[g] = total.astype(BF16)
        else:
            sd[p] = total.astype(BF16)
            d_copy(p, z_of, g).start()

    def stage_y(it):
        for s in range(2):
            p = 2 * it + s
            first_all(p, s).wait()

            def over_x(y_of):
                total = part[p, owner_rows(x * NY + y_of), :].astype(F32)
                for n in range(NX - 1):
                    total = total + dr[p, owner_rows(2 * n + y_of), :].astype(F32)
                return total

            def over_y(x_of):
                return part[p, owner_rows(x_of * NY + yh), :].astype(F32) + dr[p, owner_rows(x_of), :].astype(F32)

            if s == 0:
                sc[p, 0:SLOTS, :] = over_x(1 - yh).astype(BF16)
            else:
                for n, (_, px) in enumerate(row):
                    sc[p, n * SLOTS:(n + 1) * SLOTS, :] = over_y(px).astype(BF16)
            second_copies(p, s)
            keep[p] = over_x(yh) if s == 0 else over_y(x)

    def stage_d(it, own):
        for s in range(2):
            p = 2 * it + s
            second_all(p, s).wait()
            total = keep[p]
            for n in range((6, 4)[s], 7):
                total = total + dr[p, n * SLOTS:(n + 1) * SLOTS, :].astype(F32)
            deliver(it, s, total, own)

    def stage_o(it, own):
        for s in range(2):
            p = 2 * it + s
            o_all(p).wait()
            total = part[p, owner_rows(owner), :].astype(F32)
            for n in range(OWN - 1):
                total = total + dr[p, n * SLOTS:(n + 1) * SLOTS, :].astype(F32)
            deliver(it, s, total, own)

    def step(it, carry):
        k = it - 1

        @pl.when(it == 1)
        def _():
            ring_begin(2)
            ring_begin(3)
            w_forward(2)

        @pl.when(it == 2)
        def _():
            w_forward(3)
            w_finish(2)
            project(2)

        @pl.when(it == 3)
        def _():
            w_finish(3)
            project(3)
            w_sent(2, (0, 1))
            w_sent(3, (0, 1))
            w_start(W_OUT)
            for n in range(5):
                back_copy(2, n).start()

        @pl.when(it == 10)
        def _():
            w_forward(W_OUT)

        @pl.when((it >= 1) & (it < STEPS - 1))
        def _():
            for side in range(2):
                z_of, g = piece(it, side)
                ring(side, k, z_of, g).wait_recv()

        @pl.when((it >= 1) & (k < 10))
        def _():
            z_of, g = piece(it, 0)
            ring(0, k + 4, z_of, g).start()

        @pl.when((it >= 1) & (k < 8))
        def _():
            z_of, g = piece(it, 1)
            ring(1, k + 4, z_of, g).start()

        @pl.when((k == 10) | (k == 11))
        def _():
            z_of, g = piece(it, 1)
            ring(1, k + 2, z_of, g).start()

        @pl.when((it >= LAG) & (it < CUT + LAG))
        def _():
            stage_y(it - LAG)

        @pl.when(it == LAG + LAG - 1)
        def _():
            stage_d(0, True)

        @pl.when((it > LAG + LAG - 1) & (it < CUT + LAG + LAG - 1))
        def _():
            stage_d(it - (LAG + LAG - 1), False)

        for side in range(2):
            z_of, g = piece(it, side)
            p = 2 * it + side
            attend(z_of, g, p)

        @pl.when(it < CUT)
        def _():
            for side in range(2):
                first_copies(2 * it + side, side)

        @pl.when(it >= CUT)
        def _():
            for side in range(2):
                for n in range(OWN - 1):
                    o_copy(2 * it + side, n).start()

        return carry

    lax.fori_loop(0, STEPS, step, 0)

    for it in range(STEPS - LAG, CUT):
        stage_y(it)
    for it in range(STEPS - (LAG + LAG - 1), CUT):
        stage_d(it, False)
    for it in range(CUT, STEPS - 1):
        stage_o(it, False)
    w_finish(W_OUT)
    for n in range(5):
        back_arrived(2, n)
    gates = silu(pg[0:SLOTS, :] + rg[0] + rg[1] + rg[2])
    stage_o(STEPS - 1, True)
    remote(rd, rd, x_send.at[0], d_recv, mirror).wait_recv()
    mixed = jnp.concatenate(
        [rown[g].astype(F32) + sum(rd[n, g].astype(F32) for n in range(NZ - 1)) for g in range(GROUPS)], axis=1
    )
    gated = (normed(mixed).astype(BF16).astype(F32) * gates).astype(BF16)
    projected = jnp.dot(gated, wo[...], preferred_element_type=F32)
    out_ref[...] = (cand_ref[...].astype(F32) + projected).astype(BF16)

    for n in range(len(pieces)):
        w_sent(n, (2, 3, 4, 5) if n < W_OUT else range(6))
    for n, (peer, _) in enumerate(flat):
        remote(st1.at[owner], st1.at[owner], st_send.at[0, n], st1_recv.at[owner], peer).wait_send()
    for n, (peer, _) in enumerate(column):
        remote(st2.at[z], st2.at[z], st_send.at[1, n], st2_recv.at[z], peer).wait_send()
    for n in range(5):
        in_copy(n).wait_send()
        back_copy(1, n).wait_send()
        back_copy(2, n).wait_send()
    for g in range(GROUPS):
        q_all(g).wait_send()

    def ring_sent(n, carry):
        for side in range(2):
            ring(side, n, z, 0).wait_send()
        return carry

    lax.fori_loop(0, 14, ring_sent, 0)

    def d_sent(n, carry):
        remote(sd.at[n], rd.at[0, 0], d_send.at[n], d_recv, mirror).wait_send()
        return carry

    lax.fori_loop(2, 2 * STEPS - 2, d_sent, 0)


def local(history, hist_len, cand_start, candidates, slot_cand, w_kv, w_qu, w_o):
    pieces = 2 * STEPS
    vmem = pl.BlockSpec(memory_space=pltpu.VMEM)
    smem = pl.BlockSpec(memory_space=pltpu.SMEM)
    anywhere = pl.BlockSpec(memory_space=pl.ANY)
    dma = pltpu.SemaphoreType.DMA
    out = pl.pallas_call(
        kernel,
        out_shape=jax.ShapeDtypeStruct((SLOTS, WIDTH), BF16),
        in_specs=[smem, smem, vmem, vmem, vmem, anywhere, anywhere, anywhere],
        out_specs=vmem,
        scratch_shapes=[
            pltpu.VMEM((QUARTER, 2 * WIDTH), BF16),
            pltpu.VMEM((WIDTH, 2 * WIDTH), BF16),
            pltpu.VMEM((WIDTH, WIDTH), BF16),
            pltpu.VMEM((SPAN, WIDTH), BF16),
            pltpu.VMEM((4, SLOTS, QUARTER), BF16),
            pltpu.VMEM((4 * SLOTS, QUARTER), BF16),
            pltpu.VMEM((4 * SLOTS, WIDTH), F32),
            pltpu.VMEM((4 * SLOTS, WIDTH), F32),
            pltpu.VMEM((3, SLOTS, WIDTH), F32),
            pltpu.VMEM((3, SLOTS, WIDTH), F32),
            pltpu.VMEM((GROUPS, BLOCKS, WIDE, HEADS * KBLK), BF16),
            pltpu.VMEM((GROUPS, BLOCKS, HEADS * KBLK, WIDE), BF16),
            pltpu.VMEM((NZ, GROUPS, ROWS, WIDE), BF16),
            pltpu.VMEM((NZ, BLOCKS, ROWS, 128), BF16),
            pltpu.VMEM((OWN, 8, 128), F32),
            pltpu.VMEM((NZ, 8, 128), F32),
            pltpu.VMEM((pieces, ROWS, WIDE), BF16),
            pltpu.VMEM((pieces, (OWN - 1) * SLOTS, WIDE), BF16),
            pltpu.VMEM((pieces, (NX - 1) * SLOTS, WIDE), BF16),
            pltpu.VMEM((pieces, SLOTS, WIDE), F32),
            pltpu.VMEM((pieces, SLOTS, WIDE), BF16),
            pltpu.VMEM((NZ - 1, GROUPS, SLOTS, WIDE), BF16),
            pltpu.VMEM((GROUPS, SLOTS, WIDE), BF16),
            dma((1 + GROUPS, 6)), dma((1 + GROUPS, 6)), dma((1 + GROUPS, 2)),
            dma((3, 5)), dma((3, 5)), dma,
            dma((2, 7)), dma((OWN,)), dma((NZ,)),
            dma((GROUPS,)), dma((GROUPS,)),
            dma((2, 14)), dma((2, 14)),
            dma((pieces,)), dma((pieces,)),
            dma((pieces,)), dma((pieces,)),
            dma((pieces,)), dma,
        ],
        compiler_params=pltpu.CompilerParams(
            collective_id=0, has_side_effects=True, vmem_limit_bytes=60 * 2**20
        ),
    )(hist_len, cand_start, slot_cand, history[0], candidates[0], w_kv, w_qu, w_o)
    return out[None]


def solution(mesh):
    in_specs = (
        P("user", "seq", None),
        P("user"),
        P("user", None),
        P("user", "seq", None),
        P("user", "seq"),
        P("user", None),
        P("user", None),
        P("user", None),
    )
    out_specs = P("user", "seq", None)
    return jax.shard_map(local, mesh=mesh, in_specs=in_specs, out_specs=out_specs, check_vma=False)
```

```python
import jax
import jax.numpy as jnp
from jax import lax
from jax.experimental import pallas as pl
from jax.experimental.pallas import tpu as pltpu
from jax.sharding import PartitionSpec as P

MESH = pl.DeviceIdType.MESH
F32 = jnp.float32
BF16 = jnp.bfloat16

NX, NY, NZ = 4, 2, 8
SLOTS = 32
OWN = NX * NY
ROWS = OWN * SLOTS
WIDTH = 1024
WIDE = 256
GROUPS = WIDTH // WIDE
HEADS = 8
HEAD = 32
SPAN = 512
KBLK = 128
BLOCKS = SPAN // KBLK
CB = 128
STEPS = 16
CUT = 12
LAG = 4
QUARTER = 256


def silu(v):
    half = 0.5 * v
    return half + half * jnp.tanh(half)


def normed(rows):
    rows = rows.astype(F32)
    center = rows - jnp.mean(rows, axis=-1, keepdims=True)
    spread = jnp.mean(center * center, axis=-1, keepdims=True)
    return center * lax.rsqrt(spread + 1e-05)


def kernel(
    len_ref, start_ref, slot_ref, hist_ref, cand_ref, wkv_hbm, wqu_hbm, wo_hbm, out_ref,
    wqu, wkv, wo, nhist, ncand, cin, pq, pg, rq, rg, keys, vals, qall, masks,
    st1, st2, part, dr, sc, keep, sd, rd, rown,
    w_send, w_recv, w_local, p_send, p_recv, p_local, st_send, st1_recv, st2_recv, q_send, q_recv,
    ring_send, ring_recv, x_send, x_recv, y_send, y_recv, d_send, d_recv,
):
    seq = lax.axis_index("seq")
    user = lax.axis_index("user")
    yh = lax.div(seq, NZ * NX)
    z = lax.rem(lax.div(seq, NX), NZ)
    x = lax.rem(seq, NX)
    yl = lax.div(user, 2)
    core = lax.rem(user, 2)
    owner = x * NY + yh

    def seq_of(y_, z_, x_):
        return y_ * (NZ * NX) + z_ * NX + x_

    sib_user = user + 1 - 2 * core
    opp_user = (1 - yl) * 2 + core
    sibling = (seq, sib_user)
    near = (seq, opp_user)
    cross = (seq_of(1 - yh, z, x), opp_user)
    mirror = (seq_of(1 - yh, z, x), user)
    opposite = [(s_, (1 - yl) * 2 + k) for s_ in (seq, seq_of(1 - yh, z, x)) for k in range(2)]
    up_z = (seq_of(yh, lax.rem(z + 1, NZ), x), user)
    down_z = (seq_of(yh, lax.rem(z + NZ - 1, NZ), x), user)
    row = []
    for dx in range(1, NX):
        px = lax.rem(x + dx, NX)
        row.append(((seq_of(yh, z, px), user), px))
    flat = []
    for dx in range(NX):
        for dy in range(NY):
            if dx or dy:
                px, py = lax.rem(x + dx, NX), lax.rem(yh + dy, NY)
                flat.append(((seq_of(py, z, px), user), px * NY + py))
    column = []
    for dz in range(1, NZ):
        pz = lax.rem(z + dz, NZ)
        column.append(((seq_of(yh, pz, x), user), pz))

    barrier = pltpu.get_barrier_semaphore()
    peers = [sibling] + opposite + [p for p, _ in flat] + [p for p, _ in column]
    for peer in peers:
        pl.semaphore_signal(barrier, inc=1, device_id=peer, device_id_type=MESH)

    slots = slot_ref[...]
    window = jnp.zeros(slots.shape, F32)
    for c in range(start_ref.shape[1]):
        begin = start_ref[0, c].astype(F32)
        window = window + jnp.where((slots >= c * CB) & (slots < (c + 1) * CB), begin, 0.0)
    st1[owner] = jnp.zeros((8, 128), F32)
    st1[owner, 0:1, 0:SLOTS] = window
    pltpu.make_async_copy(wqu_hbm, wqu, p_local).start()
    rows = normed(cand_ref[...]).astype(BF16)
    for u in range(4):
        ncand[u] = rows[:, u * QUARTER:(u + 1) * QUARTER]
    cin[0:SLOTS, :] = ncand[user]

    def clear(n, carry):
        keys[lax.div(n, BLOCKS), lax.rem(n, BLOCKS)] = jnp.zeros((WIDE, HEADS * KBLK), BF16)
        vals[lax.div(n, BLOCKS), lax.rem(n, BLOCKS)] = jnp.zeros((HEADS * KBLK, WIDE), BF16)
        return carry

    lax.fori_loop(0, GROUPS * BLOCKS, clear, 0)
    pl.semaphore_wait(barrier, len(peers))

    def remote(src, dst, send, recv, device):
        return pltpu.make_async_remote_copy(
            src_ref=src, dst_ref=dst, send_sem=send, recv_sem=recv, device_id=device, device_id_type=MESH
        )

    def halves(hbm, lo, cols, dst):
        return tuple((hbm, lo + s * (cols // 2), dst, s * (cols // 2), cols // 2) for s in range(2))

    pieces = []
    for g in range(GROUPS):
        pieces.append(tuple((wkv_hbm, s * WIDTH + g * WIDE, wkv, s * WIDTH + g * WIDE, WIDE) for s in range(2)))
    pieces += [halves(wo_hbm, 0, WIDTH, wo)]
    W_OUT = GROUPS

    def own_rows(index):
        return pl.ds(pl.multiple_of(index * QUARTER, QUARTER), QUARTER)

    def w_copy(n, kind):
        hbm, lo, dst, at, cols = pieces[n][kind % 2]
        sems = (w_send.at[n, kind], w_recv.at[n, kind])
        if kind < 4:
            target = (near, cross, sibling, sibling)[kind]
            return remote(hbm.at[:, pl.ds(lo, cols)], dst.at[own_rows(user), pl.ds(at, cols)], *sems, target)
        ref = dst.at[own_rows(opp_user), pl.ds(at, cols)]
        return remote(ref, ref, *sems, sibling)

    def w_mine(n, s):
        hbm, lo, dst, at, cols = pieces[n][s]
        return pltpu.make_async_copy(hbm.at[:, pl.ds(lo, cols)], dst.at[own_rows(user), pl.ds(at, cols)], w_local.at[n, s])

    def w_start(n):
        for kind in range(4):
            w_copy(n, kind).start()
        for s in range(2):
            w_mine(n, s).start()

    def w_arrived(n, kind):
        _, _, dst, at, cols = pieces[n][kind % 2]
        rows = (opp_user, sib_user, (1 - yl) * 2 + 1 - core)[kind // 2]
        ref = dst.at[own_rows(rows), pl.ds(at, cols)]
        remote(ref, ref, w_send.at[n, kind], w_recv.at[n, kind], sibling).wait_recv()

    def w_forward(n):
        for kind in (0, 1):
            w_arrived(n, kind)
            w_copy(n, kind + 4).start()

    def w_finish(n):
        for s in range(2):
            w_mine(n, s).wait()
        for kind in range(2, 6):
            w_arrived(n, kind)

    def w_sent(n, kinds):
        for kind in kinds:
            w_copy(n, kind).wait_send()

    half = SLOTS // 2
    near_at = pl.ds(pl.multiple_of(2 * SLOTS + half * core, half), half)
    cross_at = pl.ds(pl.multiple_of(3 * SLOTS + half * core, half), half)

    def in_copy(n):
        if n == 0:
            return remote(ncand.at[sib_user], cin.at[pl.ds(SLOTS, SLOTS), :], p_send.at[0, 0], p_recv.at[0, 0], sibling)
        far, k = divmod(n - 1, 2)
        return remote(
            ncand.at[(1 - yl) * 2 + k, pl.ds(far * half, half), :], cin.at[cross_at if far else near_at, :],
            p_send.at[0, n], p_recv.at[0, 1 + 2 * far + core], opposite[n - 1],
        )

    def in_arrived(n):
        size = SLOTS if n == 0 else half
        ref = cin.at[pl.ds(0 if n == 0 else 2 * SLOTS, size), :]
        remote(ref, ref, p_send.at[0, n], p_recv.at[0, n], sibling).wait_recv()

    def back_copy(m, n):
        src, dst = ((pq, rq), (pg, rg))[m - 1]
        if n == 0:
            return remote(src.at[pl.ds(SLOTS, SLOTS), :], dst.at[0], p_send.at[m, 0], p_recv.at[m, 0], sibling)
        far, k = divmod(n - 1, 2)
        return remote(
            src.at[pl.ds((2 + far) * SLOTS + k * half, half), :], dst.at[1 + core, pl.ds(far * half, half), :],
            p_send.at[m, n], p_recv.at[m, 1 + 2 * far + core], opposite[n - 1],
        )

    def back_arrived(m, n):
        dst = (rq, rg)[m - 1]
        ref = dst.at[0] if n == 0 else dst.at[1, pl.ds(0, half), :]
        remote(ref, ref, p_send.at[m, n], p_recv.at[m, n], sibling).wait_recv()

    for n in range(5):
        in_copy(n).start()
    w_start(0)
    w_start(1)
    for n, (peer, _) in enumerate(flat):
        remote(st1.at[owner], st1.at[owner], st_send.at[0, n], st1_recv.at[owner], peer).start()

    pltpu.make_async_copy(wqu_hbm, wqu, p_local).wait()
    for n in range(5):
        in_arrived(n)
    pq[...] = jnp.dot(cin[...], wqu[:, :WIDTH], preferred_element_type=F32)
    for n in range(5):
        back_copy(1, n).start()

    def norm_rows(n, carry):
        rows = pl.ds(pl.multiple_of(n * 64, 64), 64)
        nhist[rows, :] = normed(hist_ref[rows, :]).astype(BF16)
        return carry

    lax.fori_loop(0, SPAN // 64, norm_rows, 0)

    for n, (peer, o) in enumerate(flat):
        remote(st1.at[o], st1.at[o], st_send.at[0, n], st1_recv.at[o], peer).wait_recv()
    st2[z] = jnp.concatenate([st1[o, 0:1, :] for o in range(OWN)], axis=0)
    for n, (peer, _) in enumerate(column):
        remote(st2.at[z], st2.at[z], st_send.at[1, n], st2_recv.at[z], peer).start()

    w_sent(0, (0, 1))
    w_start(2)

    for n in range(5):
        back_arrived(1, n)
    queries = silu(pq[0:SLOTS, :] + rq[0] + rq[1] + rq[2]).astype(BF16)
    mine = pl.ds(pl.multiple_of(owner * SLOTS, SLOTS), SLOTS)

    def q_copy(g, n):
        ref = qall.at[z, g, mine, :]
        return remote(ref, ref, q_send.at[g], q_recv.at[g], flat[n][0])

    others = pl.ds(0, (OWN - 1) * SLOTS)

    def q_all(g):
        ref = qall.at[z, g, others, :]
        return remote(ref, ref, q_send.at[g], q_recv.at[g], mirror)

    for g in range(GROUPS):
        qall[z, g, mine, :] = queries[:, g * WIDE:(g + 1) * WIDE]
    for g in range(2):
        for n in range(OWN - 1):
            q_copy(g, n).start()

    def ring(side, index, z_of, g):
        ref = qall.at[z_of, g]
        return remote(ref, ref, ring_send.at[side, index], ring_recv.at[side, index], up_z if side == 0 else down_z)

    def ring_begin(g):
        q_all(g).wait_recv()
        ring(0, g, z, g).start()
        ring(1, g, z, g).start()

    def project(g):
        place = lax.broadcasted_iota(jnp.int32, (SPAN, WIDE), 0) + seq * SPAN
        exists = jnp.where(place < len_ref[0], 0.5, 0.0)
        spot = lax.broadcasted_iota(jnp.int32, (KBLK, 128), 1)
        k = silu(jnp.dot(nhist[...], wkv[:, g * WIDE:(g + 1) * WIDE], preferred_element_type=F32))
        k = k.astype(BF16).astype(F32) * exists
        kt = k.T.astype(BF16)
        for j in range(BLOCKS):
            for h in range(HEADS):
                keys[g, j, h * HEAD:(h + 1) * HEAD, h * KBLK:(h + 1) * KBLK] = (
                    kt[h * HEAD:(h + 1) * HEAD, j * KBLK:(j + 1) * KBLK]
                )
        v = silu(jnp.dot(nhist[...], wkv[:, WIDTH + g * WIDE:WIDTH + (g + 1) * WIDE], preferred_element_type=F32))
        for j in range(BLOCKS):
            for h in range(HEADS):
                side, at = (h * HEAD) // 128 * 128, (h * HEAD) % 128
                own = v[j * KBLK:(j + 1) * KBLK, side:side + 128]
                own = jnp.where((spot >= at) & (spot < at + HEAD), own, 0.0).astype(BF16)
                vals[g, j, h * KBLK:(h + 1) * KBLK, side:side + 128] = own

    w_forward(0)
    w_sent(1, (0, 1))
    w_start(3)
    w_forward(1)
    for g in range(2, GROUPS):
        for n in range(OWN - 1):
            q_copy(g, n).start()
    pg[...] = jnp.dot(cin[...], wqu[:, WIDTH:], preferred_element_type=F32)
    w_finish(0)
    project(0)
    for n, (peer, pz) in enumerate(column):
        remote(st2.at[pz], st2.at[pz], st_send.at[1, n], st2_recv.at[pz], peer).wait_recv()
    lane = lax.broadcasted_iota(jnp.int32, (SLOTS, 128), 1)
    line = lax.broadcasted_iota(jnp.int32, (SLOTS, 128), 0)
    first = (seq * BLOCKS).astype(F32)

    def make_masks(n, carry):
        tile = st2[n]
        for o in range(OWN):
            spread = jnp.broadcast_to(tile[o:o + 1, :], (SLOTS, 128))
            begin = jnp.sum(jnp.where(lane == line, spread, 0.0), axis=1, keepdims=True)
            begin = jnp.broadcast_to(begin, (SLOTS, 128))
            for j in range(BLOCKS):
                masks[n, j, o * SLOTS:(o + 1) * SLOTS, :] = jnp.where(begin <= first + j, 1.0, 0.0).astype(BF16)
        return carry

    lax.fori_loop(0, NZ, make_masks, 0)

    ring_begin(0)
    w_finish(1)
    project(1)
    ring_begin(1)

    def piece(it, side):
        ahead = lax.div(STEPS - 1 - it, STEPS - 1)
        last = lax.div(it, STEPS - 1)
        mid = 1 - ahead - last
        k = it - 1 + ahead - last
        hop = mid * (1 + lax.div(k, GROUPS))
        if side == 0:
            return lax.rem(z + NZ - hop, NZ), mid * lax.rem(k, GROUPS) + 2 * last
        return lax.rem(z + hop, NZ), mid * (lax.rem(k, GROUPS) + 2 * lax.div(k, 12)) + ahead + 3 * last

    def attend(z_of, g, p):
        total = jnp.zeros((ROWS, WIDE), F32)
        for j in range(BLOCKS):
            mask = masks[z_of, j]
            q = qall[z_of, g] * jnp.concatenate([mask, mask], axis=1)
            for i in range(4):
                cols = slice(i * WIDE, (i + 1) * WIDE)
                s = jnp.dot(q, keys[g, j, :, cols], preferred_element_type=F32)
                w = (s + s * jnp.tanh(s)).astype(BF16)
                total = total + jnp.dot(w, vals[g, j, cols, :], preferred_element_type=F32)
        part[p] = total.astype(BF16)

    def owner_rows(o):
        return pl.ds(pl.multiple_of(o * SLOTS, SLOTS), SLOTS)

    def places(n, count):
        return pl.ds(n * SLOTS, count * SLOTS)

    def first_copies(p, s):
        if s == 0:
            for n, (peer, px) in enumerate(row):
                rows = pl.ds(pl.multiple_of(px * (NY * SLOTS), NY * SLOTS), NY * SLOTS)
                remote(part.at[p, rows, :], dr.at[p, places(2 * n, 2), :], x_send.at[p], x_recv.at[p], peer).start()
        else:
            for n in range(NX):
                rows = owner_rows(n * NY + 1 - yh)
                remote(part.at[p, rows, :], dr.at[p, places(n, 1), :], x_send.at[p], x_recv.at[p], mirror).start()

    def first_all(p, s):
        ref = dr.at[p, places(0, (6, 4)[s]), :]
        return remote(ref, ref, x_send.at[p], x_recv.at[p], mirror)

    def second_copies(p, s):
        if s == 0:
            src = sc.at[p, places(0, 1), :]
            remote(src, dr.at[p, places(6, 1), :], y_send.at[p], y_recv.at[p], mirror).start()
        else:
            for n, (peer, _) in enumerate(row):
                src = sc.at[p, places(n, 1), :]
                remote(src, dr.at[p, places(4 + n, 1), :], y_send.at[p], y_recv.at[p], peer).start()

    def second_all(p, s):
        ref = dr.at[p, places(6, 1) if s == 0 else places(4, 3), :]
        return remote(ref, ref, y_send.at[p], y_recv.at[p], mirror)

    def o_copy(p, n):
        peer, o = flat[n]
        return remote(part.at[p, owner_rows(o), :], dr.at[p, pl.ds(n * SLOTS, SLOTS), :], x_send.at[p], x_recv.at[p], peer)

    def o_all(p):
        ref = dr.at[p]
        return remote(ref, ref, x_send.at[p], x_recv.at[p], mirror)

    def d_copy(p, z_of, g):
        hop = lax.rem(z + NZ - z_of, NZ) - 1
        return remote(sd.at[p], rd.at[hop, g], d_send.at[p], d_recv, (seq_of(yh, z_of, x), user))

    def deliver(it, s, total, own):
        p = 2 * it + s
        z_of, g = piece(it, s)
        if own:
            rown[g] = total.astype(BF16)
        else:
            sd[p] = total.astype(BF16)
            d_copy(p, z_of, g).start()

    def stage_y(it):
        for s in range(2):
            p = 2 * it + s
            first_all(p, s).wait()

            def over_x(y_of):
                total = part[p, owner_rows(x * NY + y_of), :].astype(F32)
                for n in range(NX - 1):
                    total = total + dr[p, owner_rows(2 * n + y_of), :].astype(F32)
                return total

            def over_y(x_of):
                return part[p, owner_rows(x_of * NY + yh), :].astype(F32) + dr[p, owner_rows(x_of), :].astype(F32)

            if s == 0:
                sc[p, 0:SLOTS, :] = over_x(1 - yh).astype(BF16)
            else:
                for n, (_, px) in enumerate(row):
                    sc[p, n * SLOTS:(n + 1) * SLOTS, :] = over_y(px).astype(BF16)
            second_copies(p, s)
            keep[p] = over_x(yh) if s == 0 else over_y(x)

    def stage_d(it, own):
        for s in range(2):
            p = 2 * it + s
            second_all(p, s).wait()
            total = keep[p]
            for n in range((6, 4)[s], 7):
                total = total + dr[p, n * SLOTS:(n + 1) * SLOTS, :].astype(F32)
            deliver(it, s, total, own)

    def stage_o(it, own):
        for s in range(2):
            p = 2 * it + s
            o_all(p).wait()
            total = part[p, owner_rows(owner), :].astype(F32)
            for n in range(OWN - 1):
                total = total + dr[p, n * SLOTS:(n + 1) * SLOTS, :].astype(F32)
            deliver(it, s, total, own)

    def step(it, carry):
        k = it - 1

        @pl.when(it == 1)
        def _():
            ring_begin(2)
            w_forward(2)

        @pl.when(it == 2)
        def _():
            ring_begin(3)
            w_forward(3)
            w_finish(2)
            project(2)

        @pl.when(it == 3)
        def _():
            w_finish(3)
            project(3)
            w_sent(2, (0, 1))
            w_sent(3, (0, 1))
            w_start(W_OUT)

        @pl.when(it == 9)
        def _():
            for n in range(5):
                back_copy(2, n).start()

        @pl.when(it == 10)
        def _():
            w_forward(W_OUT)

        @pl.when((it >= 1) & (it < STEPS - 1))
        def _():
            for side in range(2):
                z_of, g = piece(it, side)
                ring(side, k, z_of, g).wait_recv()

        def pass_on(side, item):
            z_of, g = piece(item + 1, side)
            ring(side, item + 4, z_of, g).start()

        @pl.when(it == 2)
        def _():
            pass_on(0, 0)
            pass_on(1, 0)

        @pl.when(it == 3)
        def _():
            for item in (1, 2):
                pass_on(0, item)
                pass_on(1, item)

        @pl.when((it >= 4) & (k < 10))
        def _():
            pass_on(0, k)

        @pl.when((it >= 4) & (k < 8))
        def _():
            pass_on(1, k)

        @pl.when((k == 10) | (k == 11))
        def _():
            z_of, g = piece(it, 1)
            ring(1, k + 2, z_of, g).start()

        @pl.when((it >= LAG) & (it < CUT + LAG))
        def _():
            stage_y(it - LAG)

        @pl.when(it == LAG + LAG - 1)
        def _():
            stage_d(0, True)

        @pl.when((it > LAG + LAG - 1) & (it < CUT + LAG + LAG - 1))
        def _():
            stage_d(it - (LAG + LAG - 1), False)

        @pl.when(it == STEPS - 1)
        def _():
            stage_o(CUT, False)

        for side in range(2):
            z_of, g = piece(it, side)
            p = 2 * it + side
            attend(z_of, g, p)

        @pl.when(it < CUT)
        def _():
            for side in range(2):
                first_copies(2 * it + side, side)

        @pl.when(it >= CUT)
        def _():
            for side in range(2):
                for n in range(OWN - 1):
                    o_copy(2 * it + side, n).start()

        return carry

    lax.fori_loop(0, STEPS, step, 0)

    for it in range(STEPS - LAG, CUT):
        stage_y(it)
    for it in range(STEPS - (LAG + LAG - 1), CUT):
        stage_d(it, False)
    for it in range(CUT + 1, STEPS - 1):
        stage_o(it, False)
    w_finish(W_OUT)
    for n in range(5):
        back_arrived(2, n)
    gates = silu(pg[0:SLOTS, :] + rg[0] + rg[1] + rg[2])
    stage_o(STEPS - 1, True)
    remote(rd, rd, x_send.at[0], d_recv, mirror).wait_recv()
    mixed = jnp.concatenate(
        [rown[g].astype(F32) + sum(rd[n, g].astype(F32) for n in range(NZ - 1)) for g in range(GROUPS)], axis=1
    )
    gated = (normed(mixed).astype(BF16).astype(F32) * gates).astype(BF16)
    projected = jnp.dot(gated, wo[...], preferred_element_type=F32)
    out_ref[...] = (cand_ref[...].astype(F32) + projected).astype(BF16)

    for n in range(len(pieces)):
        w_sent(n, (2, 3, 4, 5) if n < W_OUT else range(6))
    for n, (peer, _) in enumerate(flat):
        remote(st1.at[owner], st1.at[owner], st_send.at[0, n], st1_recv.at[owner], peer).wait_send()
    for n, (peer, _) in enumerate(column):
        remote(st2.at[z], st2.at[z], st_send.at[1, n], st2_recv.at[z], peer).wait_send()
    for n in range(5):
        in_copy(n).wait_send()
        back_copy(1, n).wait_send()
        back_copy(2, n).wait_send()
    for g in range(GROUPS):
        q_all(g).wait_send()

    def ring_sent(n, carry):
        for side in range(2):
            ring(side, n, z, 0).wait_send()
        return carry

    lax.fori_loop(0, 14, ring_sent, 0)

    def d_sent(n, carry):
        remote(sd.at[n], rd.at[0, 0], d_send.at[n], d_recv, mirror).wait_send()
        return carry

    lax.fori_loop(2, 2 * STEPS - 2, d_sent, 0)


def local(history, hist_len, cand_start, candidates, slot_cand, w_kv, w_qu, w_o):
    pieces = 2 * STEPS
    vmem = pl.BlockSpec(memory_space=pltpu.VMEM)
    smem = pl.BlockSpec(memory_space=pltpu.SMEM)
    anywhere = pl.BlockSpec(memory_space=pl.ANY)
    dma = pltpu.SemaphoreType.DMA
    out = pl.pallas_call(
        kernel,
        out_shape=jax.ShapeDtypeStruct((SLOTS, WIDTH), BF16),
        in_specs=[smem, smem, vmem, vmem, vmem, anywhere, anywhere, anywhere],
        out_specs=vmem,
        scratch_shapes=[
            pltpu.VMEM((QUARTER, 2 * WIDTH), BF16),
            pltpu.VMEM((WIDTH, 2 * WIDTH), BF16),
            pltpu.VMEM((WIDTH, WIDTH), BF16),
            pltpu.VMEM((SPAN, WIDTH), BF16),
            pltpu.VMEM((4, SLOTS, QUARTER), BF16),
            pltpu.VMEM((4 * SLOTS, QUARTER), BF16),
            pltpu.VMEM((4 * SLOTS, WIDTH), F32),
            pltpu.VMEM((4 * SLOTS, WIDTH), F32),
            pltpu.VMEM((3, SLOTS, WIDTH), F32),
            pltpu.VMEM((3, SLOTS, WIDTH), F32),
            pltpu.VMEM((GROUPS, BLOCKS, WIDE, HEADS * KBLK), BF16),
            pltpu.VMEM((GROUPS, BLOCKS, HEADS * KBLK, WIDE), BF16),
            pltpu.VMEM((NZ, GROUPS, ROWS, WIDE), BF16),
            pltpu.VMEM((NZ, BLOCKS, ROWS, 128), BF16),
            pltpu.VMEM((OWN, 8, 128), F32),
            pltpu.VMEM((NZ, 8, 128), F32),
            pltpu.VMEM((pieces, ROWS, WIDE), BF16),
            pltpu.VMEM((pieces, (OWN - 1) * SLOTS, WIDE), BF16),
            pltpu.VMEM((pieces, (NX - 1) * SLOTS, WIDE), BF16),
            pltpu.VMEM((pieces, SLOTS, WIDE), F32),
            pltpu.VMEM((pieces, SLOTS, WIDE), BF16),
            pltpu.VMEM((NZ - 1, GROUPS, SLOTS, WIDE), BF16),
            pltpu.VMEM((GROUPS, SLOTS, WIDE), BF16),
            dma((1 + GROUPS, 6)), dma((1 + GROUPS, 6)), dma((1 + GROUPS, 2)),
            dma((3, 5)), dma((3, 5)), dma,
            dma((2, 7)), dma((OWN,)), dma((NZ,)),
            dma((GROUPS,)), dma((GROUPS,)),
            dma((2, 14)), dma((2, 14)),
            dma((pieces,)), dma((pieces,)),
            dma((pieces,)), dma((pieces,)),
            dma((pieces,)), dma,
        ],
        compiler_params=pltpu.CompilerParams(
            collective_id=0, has_side_effects=True, vmem_limit_bytes=60 * 2**20
        ),
    )(hist_len, cand_start, slot_cand, history[0], candidates[0], w_kv, w_qu, w_o)
    return out[None]


def solution(mesh):
    in_specs = (
        P("user", "seq", None),
        P("user"),
        P("user", None),
        P("user", "seq", None),
        P("user", "seq"),
        P("user", None),
        P("user", None),
        P("user", None),
    )
    out_specs = P("user", "seq", None)
    return jax.shard_map(local, mesh=mesh, in_specs=in_specs, out_specs=out_specs, check_vma=False)
```

```python
import jax
import jax.numpy as jnp
from jax import lax
from jax.experimental import pallas as pl
from jax.experimental.pallas import tpu as pltpu
from jax.sharding import PartitionSpec as P

MESH = pl.DeviceIdType.MESH
F32 = jnp.float32
BF16 = jnp.bfloat16

NX, NY, NZ = 4, 2, 8
SLOTS = 32
OWN = NX * NY
ROWS = OWN * SLOTS
WIDTH = 1024
WIDE = 256
GROUPS = WIDTH // WIDE
HEADS = 8
HEAD = 32
SPAN = 512
KBLK = 128
BLOCKS = SPAN // KBLK
CB = 128
STEPS = 16
CUT = 12
LAG = 4
QUARTER = 256


def silu(v):
    half = 0.5 * v
    return half + half * jnp.tanh(half)


def normed(rows):
    rows = rows.astype(F32)
    center = rows - jnp.mean(rows, axis=-1, keepdims=True)
    spread = jnp.mean(center * center, axis=-1, keepdims=True)
    return center * lax.rsqrt(spread + 1e-05)


def kernel(
    len_ref, start_ref, slot_ref, hist_ref, cand_ref, wkv_hbm, wqu_hbm, wo_hbm, out_ref,
    wqu, wkv, wo, nhist, ncand, cin, pq, pg, rq, rg, keys, vals, qall, masks,
    st1, st2, part, dr, sc, keep, sd, rd, rown,
    w_send, w_recv, w_local, p_send, p_recv, p_local, st_send, st1_recv, st2_recv, q_send, q_recv,
    ring_send, ring_recv, x_send, x_recv, y_send, y_recv, d_send, d_recv,
):
    seq = lax.axis_index("seq")
    user = lax.axis_index("user")
    yh = lax.div(seq, NZ * NX)
    z = lax.rem(lax.div(seq, NX), NZ)
    x = lax.rem(seq, NX)
    yl = lax.div(user, 2)
    core = lax.rem(user, 2)
    owner = x * NY + yh

    def seq_of(y_, z_, x_):
        return y_ * (NZ * NX) + z_ * NX + x_

    sib_user = user + 1 - 2 * core
    opp_user = (1 - yl) * 2 + core
    sibling = (seq, sib_user)
    near = (seq, opp_user)
    cross = (seq_of(1 - yh, z, x), opp_user)
    mirror = (seq_of(1 - yh, z, x), user)
    opposite = [(s_, (1 - yl) * 2 + k) for s_ in (seq, seq_of(1 - yh, z, x)) for k in range(2)]
    up_z = (seq_of(yh, lax.rem(z + 1, NZ), x), user)
    down_z = (seq_of(yh, lax.rem(z + NZ - 1, NZ), x), user)
    row = []
    for dx in range(1, NX):
        px = lax.rem(x + dx, NX)
        row.append(((seq_of(yh, z, px), user), px))
    flat = []
    for dx in range(NX):
        for dy in range(NY):
            if dx or dy:
                px, py = lax.rem(x + dx, NX), lax.rem(yh + dy, NY)
                flat.append(((seq_of(py, z, px), user), px * NY + py))
    column = []
    for dz in range(1, NZ):
        pz = lax.rem(z + dz, NZ)
        column.append(((seq_of(yh, pz, x), user), pz))

    barrier = pltpu.get_barrier_semaphore()
    peers = [sibling] + opposite + [p for p, _ in flat] + [p for p, _ in column]
    for peer in peers:
        pl.semaphore_signal(barrier, inc=1, device_id=peer, device_id_type=MESH)

    slots = slot_ref[...]
    window = jnp.zeros(slots.shape, F32)
    for c in range(start_ref.shape[1]):
        begin = start_ref[0, c].astype(F32)
        window = window + jnp.where((slots >= c * CB) & (slots < (c + 1) * CB), begin, 0.0)
    st1[owner] = jnp.zeros((8, 128), F32)
    st1[owner, 0:1, 0:SLOTS] = window
    pltpu.make_async_copy(wqu_hbm, wqu, p_local).start()
    rows = normed(cand_ref[...]).astype(BF16)
    for u in range(4):
        ncand[u] = rows[:, u * QUARTER:(u + 1) * QUARTER]
    cin[0:SLOTS, :] = ncand[user]

    def clear(n, carry):
        keys[lax.div(n, BLOCKS), lax.rem(n, BLOCKS)] = jnp.zeros((WIDE, HEADS * KBLK), BF16)
        vals[lax.div(n, BLOCKS), lax.rem(n, BLOCKS)] = jnp.zeros((HEADS * KBLK, WIDE), BF16)
        return carry

    lax.fori_loop(0, GROUPS * BLOCKS, clear, 0)
    pl.semaphore_wait(barrier, len(peers))

    def remote(src, dst, send, recv, device):
        return pltpu.make_async_remote_copy(
            src_ref=src, dst_ref=dst, send_sem=send, recv_sem=recv, device_id=device, device_id_type=MESH
        )

    def halves(hbm, lo, cols, dst):
        return tuple((hbm, lo + s * (cols // 2), dst, s * (cols // 2), cols // 2) for s in range(2))

    pieces = []
    for g in range(GROUPS):
        pieces.append(tuple((wkv_hbm, s * WIDTH + g * WIDE, wkv, s * WIDTH + g * WIDE, WIDE) for s in range(2)))
    pieces += [halves(wo_hbm, 0, WIDTH, wo)]
    W_OUT = GROUPS

    def own_rows(index):
        return pl.ds(pl.multiple_of(index * QUARTER, QUARTER), QUARTER)

    def w_copy(n, kind):
        hbm, lo, dst, at, cols = pieces[n][kind % 2]
        sems = (w_send.at[n, kind], w_recv.at[n, kind])
        if kind < 4:
            target = (near, cross, sibling, sibling)[kind]
            return remote(hbm.at[:, pl.ds(lo, cols)], dst.at[own_rows(user), pl.ds(at, cols)], *sems, target)
        ref = dst.at[own_rows(opp_user), pl.ds(at, cols)]
        return remote(ref, ref, *sems, sibling)

    def w_mine(n, s):
        hbm, lo, dst, at, cols = pieces[n][s]
        return pltpu.make_async_copy(hbm.at[:, pl.ds(lo, cols)], dst.at[own_rows(user), pl.ds(at, cols)], w_local.at[n, s])

    def w_start(n):
        for kind in range(4):
            w_copy(n, kind).start()
        for s in range(2):
            w_mine(n, s).start()

    def w_arrived(n, kind):
        _, _, dst, at, cols = pieces[n][kind % 2]
        rows = (opp_user, sib_user, (1 - yl) * 2 + 1 - core)[kind // 2]
        ref = dst.at[own_rows(rows), pl.ds(at, cols)]
        remote(ref, ref, w_send.at[n, kind], w_recv.at[n, kind], sibling).wait_recv()

    def w_forward(n):
        for kind in (0, 1):
            w_arrived(n, kind)
            w_copy(n, kind + 4).start()

    def w_finish(n):
        for s in range(2):
            w_mine(n, s).wait()
        for kind in range(2, 6):
            w_arrived(n, kind)

    def w_sent(n, kinds):
        for kind in kinds:
            w_copy(n, kind).wait_send()

    half = SLOTS // 2
    near_at = pl.ds(pl.multiple_of(2 * SLOTS + half * core, half), half)
    cross_at = pl.ds(pl.multiple_of(3 * SLOTS + half * core, half), half)

    def in_copy(n):
        if n == 0:
            return remote(ncand.at[sib_user], cin.at[pl.ds(SLOTS, SLOTS), :], p_send.at[0, 0], p_recv.at[0, 0], sibling)
        far, k = divmod(n - 1, 2)
        return remote(
            ncand.at[(1 - yl) * 2 + k, pl.ds(far * half, half), :], cin.at[cross_at if far else near_at, :],
            p_send.at[0, n], p_recv.at[0, 1 + 2 * far + core], opposite[n - 1],
        )

    def in_arrived(n):
        size = SLOTS if n == 0 else half
        ref = cin.at[pl.ds(0 if n == 0 else 2 * SLOTS, size), :]
        remote(ref, ref, p_send.at[0, n], p_recv.at[0, n], sibling).wait_recv()

    def back_copy(m, n):
        src, dst = ((pq, rq), (pg, rg))[m - 1]
        if n == 0:
            return remote(src.at[pl.ds(SLOTS, SLOTS), :], dst.at[0], p_send.at[m, 0], p_recv.at[m, 0], sibling)
        far, k = divmod(n - 1, 2)
        return remote(
            src.at[pl.ds((2 + far) * SLOTS + k * half, half), :], dst.at[1 + core, pl.ds(far * half, half), :],
            p_send.at[m, n], p_recv.at[m, 1 + 2 * far + core], opposite[n - 1],
        )

    def back_arrived(m, n):
        dst = (rq, rg)[m - 1]
        ref = dst.at[0] if n == 0 else dst.at[1, pl.ds(0, half), :]
        remote(ref, ref, p_send.at[m, n], p_recv.at[m, n], sibling).wait_recv()

    for n in range(5):
        in_copy(n).start()
    w_start(0)
    w_start(1)
    for n, (peer, _) in enumerate(flat):
        remote(st1.at[owner], st1.at[owner], st_send.at[0, n], st1_recv.at[owner], peer).start()

    pltpu.make_async_copy(wqu_hbm, wqu, p_local).wait()
    for n in range(5):
        in_arrived(n)
    pq[...] = jnp.dot(cin[...], wqu[:, :WIDTH], preferred_element_type=F32).astype(BF16)
    for n in range(5):
        back_copy(1, n).start()

    def norm_rows(n, carry):
        rows = pl.ds(pl.multiple_of(n * 64, 64), 64)
        nhist[rows, :] = normed(hist_ref[rows, :]).astype(BF16)
        return carry

    lax.fori_loop(0, SPAN // 64, norm_rows, 0)

    for n, (peer, o) in enumerate(flat):
        remote(st1.at[o], st1.at[o], st_send.at[0, n], st1_recv.at[o], peer).wait_recv()
    st2[z] = jnp.concatenate([st1[o, 0:1, :] for o in range(OWN)], axis=0)
    for n, (peer, _) in enumerate(column):
        remote(st2.at[z], st2.at[z], st_send.at[1, n], st2_recv.at[z], peer).start()

    w_sent(0, (0, 1))
    w_start(2)

    for n in range(5):
        back_arrived(1, n)
    queries = silu(pq[0:SLOTS, :].astype(F32) + sum(rq[n].astype(F32) for n in range(3))).astype(BF16)
    mine = pl.ds(pl.multiple_of(owner * SLOTS, SLOTS), SLOTS)

    def q_copy(g, n):
        ref = qall.at[z, g, mine, :]
        return remote(ref, ref, q_send.at[g], q_recv.at[g], flat[n][0])

    others = pl.ds(0, (OWN - 1) * SLOTS)

    def q_all(g):
        ref = qall.at[z, g, others, :]
        return remote(ref, ref, q_send.at[g], q_recv.at[g], mirror)

    for g in range(GROUPS):
        qall[z, g, mine, :] = queries[:, g * WIDE:(g + 1) * WIDE]
    for g in range(2):
        for n in range(OWN - 1):
            q_copy(g, n).start()

    def ring(side, index, z_of, g):
        ref = qall.at[z_of, g]
        return remote(ref, ref, ring_send.at[side, index], ring_recv.at[side, index], up_z if side == 0 else down_z)

    def ring_begin(g):
        q_all(g).wait_recv()
        ring(0, g, z, g).start()
        ring(1, g, z, g).start()

    def project(g):
        place = lax.broadcasted_iota(jnp.int32, (SPAN, WIDE), 0) + seq * SPAN
        exists = jnp.where(place < len_ref[0], 0.5, 0.0)
        spot = lax.broadcasted_iota(jnp.int32, (KBLK, 128), 1)
        k = silu(jnp.dot(nhist[...], wkv[:, g * WIDE:(g + 1) * WIDE], preferred_element_type=F32))
        k = k.astype(BF16).astype(F32) * exists
        kt = k.T.astype(BF16)
        for j in range(BLOCKS):
            for h in range(HEADS):
                keys[g, j, h * HEAD:(h + 1) * HEAD, h * KBLK:(h + 1) * KBLK] = (
                    kt[h * HEAD:(h + 1) * HEAD, j * KBLK:(j + 1) * KBLK]
                )
        v = silu(jnp.dot(nhist[...], wkv[:, WIDTH + g * WIDE:WIDTH + (g + 1) * WIDE], preferred_element_type=F32))
        for j in range(BLOCKS):
            for h in range(HEADS):
                side, at = (h * HEAD) // 128 * 128, (h * HEAD) % 128
                own = v[j * KBLK:(j + 1) * KBLK, side:side + 128]
                own = jnp.where((spot >= at) & (spot < at + HEAD), own, 0.0).astype(BF16)
                vals[g, j, h * KBLK:(h + 1) * KBLK, side:side + 128] = own

    w_forward(0)
    w_sent(1, (0, 1))
    w_start(3)
    w_forward(1)
    for g in range(2, GROUPS):
        for n in range(OWN - 1):
            q_copy(g, n).start()
    pg[...] = jnp.dot(cin[...], wqu[:, WIDTH:], preferred_element_type=F32).astype(BF16)
    w_finish(0)
    project(0)
    for n, (peer, pz) in enumerate(column):
        remote(st2.at[pz], st2.at[pz], st_send.at[1, n], st2_recv.at[pz], peer).wait_recv()
    lane = lax.broadcasted_iota(jnp.int32, (SLOTS, 128), 1)
    line = lax.broadcasted_iota(jnp.int32, (SLOTS, 128), 0)
    first = (seq * BLOCKS).astype(F32)

    def make_masks(n, carry):
        tile = st2[n]
        for o in range(OWN):
            spread = jnp.broadcast_to(tile[o:o + 1, :], (SLOTS, 128))
            begin = jnp.sum(jnp.where(lane == line, spread, 0.0), axis=1, keepdims=True)
            begin = jnp.broadcast_to(begin, (SLOTS, 128))
            for j in range(BLOCKS):
                masks[n, j, o * SLOTS:(o + 1) * SLOTS, :] = jnp.where(begin <= first + j, 1.0, 0.0).astype(BF16)
        return carry

    lax.fori_loop(0, NZ, make_masks, 0)

    ring_begin(0)
    w_finish(1)
    project(1)
    ring_begin(1)

    def piece(it, side):
        ahead = lax.div(STEPS - 1 - it, STEPS - 1)
        last = lax.div(it, STEPS - 1)
        mid = 1 - ahead - last
        k = it - 1 + ahead - last
        hop = mid * (1 + lax.div(k, GROUPS))
        if side == 0:
            return lax.rem(z + NZ - hop, NZ), mid * lax.rem(k, GROUPS) + 2 * last
        return lax.rem(z + hop, NZ), mid * (lax.rem(k, GROUPS) + 2 * lax.div(k, 12)) + ahead + 3 * last

    def attend(z_of, g, p):
        total = jnp.zeros((ROWS, WIDE), F32)
        for j in range(BLOCKS):
            mask = masks[z_of, j]
            q = qall[z_of, g] * jnp.concatenate([mask, mask], axis=1)
            for i in range(4):
                cols = slice(i * WIDE, (i + 1) * WIDE)
                s = jnp.dot(q, keys[g, j, :, cols], preferred_element_type=F32)
                w = (s + s * jnp.tanh(s)).astype(BF16)
                total = total + jnp.dot(w, vals[g, j, cols, :], preferred_element_type=F32)
        part[p] = total.astype(BF16)

    def owner_rows(o):
        return pl.ds(pl.multiple_of(o * SLOTS, SLOTS), SLOTS)

    def places(n, count):
        return pl.ds(n * SLOTS, count * SLOTS)

    def first_copies(p, s):
        if s == 0:
            for n, (peer, px) in enumerate(row):
                rows = pl.ds(pl.multiple_of(px * (NY * SLOTS), NY * SLOTS), NY * SLOTS)
                remote(part.at[p, rows, :], dr.at[p, places(2 * n, 2), :], x_send.at[p], x_recv.at[p], peer).start()
        else:
            for n in range(NX):
                rows = owner_rows(n * NY + 1 - yh)
                remote(part.at[p, rows, :], dr.at[p, places(n, 1), :], x_send.at[p], x_recv.at[p], mirror).start()

    def first_all(p, s):
        ref = dr.at[p, places(0, (6, 4)[s]), :]
        return remote(ref, ref, x_send.at[p], x_recv.at[p], mirror)

    def second_copies(p, s):
        if s == 0:
            src = sc.at[p, places(0, 1), :]
            remote(src, dr.at[p, places(6, 1), :], y_send.at[p], y_recv.at[p], mirror).start()
        else:
            for n, (peer, _) in enumerate(row):
                src = sc.at[p, places(n, 1), :]
                remote(src, dr.at[p, places(4 + n, 1), :], y_send.at[p], y_recv.at[p], peer).start()

    def second_all(p, s):
        ref = dr.at[p, places(6, 1) if s == 0 else places(4, 3), :]
        return remote(ref, ref, y_send.at[p], y_recv.at[p], mirror)

    def o_copy(p, n):
        peer, o = flat[n]
        return remote(part.at[p, owner_rows(o), :], dr.at[p, pl.ds(n * SLOTS, SLOTS), :], x_send.at[p], x_recv.at[p], peer)

    def o_all(p):
        ref = dr.at[p]
        return remote(ref, ref, x_send.at[p], x_recv.at[p], mirror)

    def d_copy(p, z_of, g):
        hop = lax.rem(z + NZ - z_of, NZ) - 1
        return remote(sd.at[p], rd.at[hop, g], d_send.at[p], d_recv, (seq_of(yh, z_of, x), user))

    def deliver(it, s, total, own):
        p = 2 * it + s
        z_of, g = piece(it, s)
        if own:
            rown[g] = total.astype(BF16)
        else:
            sd[p] = total.astype(BF16)
            d_copy(p, z_of, g).start()

    def stage_y(it):
        for s in range(2):
            p = 2 * it + s
            first_all(p, s).wait()

            def over_x(y_of):
                total = part[p, owner_rows(x * NY + y_of), :].astype(F32)
                for n in range(NX - 1):
                    total = total + dr[p, owner_rows(2 * n + y_of), :].astype(F32)
                return total

            def over_y(x_of):
                return part[p, owner_rows(x_of * NY + yh), :].astype(F32) + dr[p, owner_rows(x_of), :].astype(F32)

            if s == 0:
                sc[p, 0:SLOTS, :] = over_x(1 - yh).astype(BF16)
            else:
                for n, (_, px) in enumerate(row):
                    sc[p, n * SLOTS:(n + 1) * SLOTS, :] = over_y(px).astype(BF16)
            second_copies(p, s)
            keep[p] = over_x(yh) if s == 0 else over_y(x)

    def stage_d(it, own):
        for s in range(2):
            p = 2 * it + s
            second_all(p, s).wait()
            total = keep[p]
            for n in range((6, 4)[s], 7):
                total = total + dr[p, n * SLOTS:(n + 1) * SLOTS, :].astype(F32)
            deliver(it, s, total, own)

    def stage_o(it, own):
        for s in range(2):
            p = 2 * it + s
            o_all(p).wait()
            total = part[p, owner_rows(owner), :].astype(F32)
            for n in range(OWN - 1):
                total = total + dr[p, n * SLOTS:(n + 1) * SLOTS, :].astype(F32)
            deliver(it, s, total, own)

    def step(it, carry):
        k = it - 1

        @pl.when(it == 1)
        def _():
            ring_begin(2)
            w_forward(2)

        @pl.when(it == 2)
        def _():
            ring_begin(3)
            w_forward(3)
            w_finish(2)
            project(2)

        @pl.when(it == 3)
        def _():
            w_finish(3)
            project(3)
            w_sent(2, (0, 1))
            w_sent(3, (0, 1))
            w_start(W_OUT)

        @pl.when(it == 9)
        def _():
            for n in range(5):
                back_copy(2, n).start()

        @pl.when(it == 10)
        def _():
            w_forward(W_OUT)

        @pl.when((it >= 1) & (it < STEPS - 1))
        def _():
            for side in range(2):
                z_of, g = piece(it, side)
                ring(side, k, z_of, g).wait_recv()

        def pass_on(side, item):
            z_of, g = piece(item + 1, side)
            ring(side, item + 4, z_of, g).start()

        @pl.when(it == 2)
        def _():
            pass_on(0, 0)
            pass_on(1, 0)

        @pl.when(it == 3)
        def _():
            for item in (1, 2):
                pass_on(0, item)
                pass_on(1, item)

        @pl.when((it >= 4) & (k < 10))
        def _():
            pass_on(0, k)

        @pl.when((it >= 4) & (k < 8))
        def _():
            pass_on(1, k)

        @pl.when((k == 10) | (k == 11))
        def _():
            z_of, g = piece(it, 1)
            ring(1, k + 2, z_of, g).start()

        @pl.when((it >= LAG) & (it < CUT + LAG))
        def _():
            stage_y(it - LAG)

        @pl.when(it == LAG + LAG - 1)
        def _():
            stage_d(0, True)

        @pl.when((it > LAG + LAG - 1) & (it < CUT + LAG + LAG - 1))
        def _():
            stage_d(it - (LAG + LAG - 1), False)

        @pl.when(it == STEPS - 1)
        def _():
            stage_o(CUT, False)

        for side in range(2):
            z_of, g = piece(it, side)
            p = 2 * it + side
            attend(z_of, g, p)

        @pl.when(it < CUT)
        def _():
            for side in range(2):
                first_copies(2 * it + side, side)

        @pl.when(it >= CUT)
        def _():
            for side in range(2):
                for n in range(OWN - 1):
                    o_copy(2 * it + side, n).start()

        return carry

    lax.fori_loop(0, STEPS, step, 0)

    for it in range(STEPS - LAG, CUT):
        stage_y(it)
    for it in range(STEPS - (LAG + LAG - 1), CUT):
        stage_d(it, False)
    for it in range(CUT + 1, STEPS - 1):
        stage_o(it, False)
    w_finish(W_OUT)
    for n in range(5):
        back_arrived(2, n)
    gates = silu(pg[0:SLOTS, :].astype(F32) + sum(rg[n].astype(F32) for n in range(3)))
    stage_o(STEPS - 1, True)
    remote(rd, rd, x_send.at[0], d_recv, mirror).wait_recv()
    mixed = jnp.concatenate(
        [rown[g].astype(F32) + sum(rd[n, g].astype(F32) for n in range(NZ - 1)) for g in range(GROUPS)], axis=1
    )
    gated = (normed(mixed).astype(BF16).astype(F32) * gates).astype(BF16)
    projected = jnp.dot(gated, wo[...], preferred_element_type=F32)
    out_ref[...] = (cand_ref[...].astype(F32) + projected).astype(BF16)

    for n in range(len(pieces)):
        w_sent(n, (2, 3, 4, 5) if n < W_OUT else range(6))
    for n, (peer, _) in enumerate(flat):
        remote(st1.at[owner], st1.at[owner], st_send.at[0, n], st1_recv.at[owner], peer).wait_send()
    for n, (peer, _) in enumerate(column):
        remote(st2.at[z], st2.at[z], st_send.at[1, n], st2_recv.at[z], peer).wait_send()
    for n in range(5):
        in_copy(n).wait_send()
        back_copy(1, n).wait_send()
        back_copy(2, n).wait_send()
    for g in range(GROUPS):
        q_all(g).wait_send()

    def ring_sent(n, carry):
        for side in range(2):
            ring(side, n, z, 0).wait_send()
        return carry

    lax.fori_loop(0, 14, ring_sent, 0)

    def d_sent(n, carry):
        remote(sd.at[n], rd.at[0, 0], d_send.at[n], d_recv, mirror).wait_send()
        return carry

    lax.fori_loop(2, 2 * STEPS - 2, d_sent, 0)


def local(history, hist_len, cand_start, candidates, slot_cand, w_kv, w_qu, w_o):
    pieces = 2 * STEPS
    vmem = pl.BlockSpec(memory_space=pltpu.VMEM)
    smem = pl.BlockSpec(memory_space=pltpu.SMEM)
    anywhere = pl.BlockSpec(memory_space=pl.ANY)
    dma = pltpu.SemaphoreType.DMA
    out = pl.pallas_call(
        kernel,
        out_shape=jax.ShapeDtypeStruct((SLOTS, WIDTH), BF16),
        in_specs=[smem, smem, vmem, vmem, vmem, anywhere, anywhere, anywhere],
        out_specs=vmem,
        scratch_shapes=[
            pltpu.VMEM((QUARTER, 2 * WIDTH), BF16),
            pltpu.VMEM((WIDTH, 2 * WIDTH), BF16),
            pltpu.VMEM((WIDTH, WIDTH), BF16),
            pltpu.VMEM((SPAN, WIDTH), BF16),
            pltpu.VMEM((4, SLOTS, QUARTER), BF16),
            pltpu.VMEM((4 * SLOTS, QUARTER), BF16),
            pltpu.VMEM((4 * SLOTS, WIDTH), BF16),
            pltpu.VMEM((4 * SLOTS, WIDTH), BF16),
            pltpu.VMEM((3, SLOTS, WIDTH), BF16),
            pltpu.VMEM((3, SLOTS, WIDTH), BF16),
            pltpu.VMEM((GROUPS, BLOCKS, WIDE, HEADS * KBLK), BF16),
            pltpu.VMEM((GROUPS, BLOCKS, HEADS * KBLK, WIDE), BF16),
            pltpu.VMEM((NZ, GROUPS, ROWS, WIDE), BF16),
            pltpu.VMEM((NZ, BLOCKS, ROWS, 128), BF16),
            pltpu.VMEM((OWN, 8, 128), F32),
            pltpu.VMEM((NZ, 8, 128), F32),
            pltpu.VMEM((pieces, ROWS, WIDE), BF16),
            pltpu.VMEM((pieces, (OWN - 1) * SLOTS, WIDE), BF16),
            pltpu.VMEM((pieces, (NX - 1) * SLOTS, WIDE), BF16),
            pltpu.VMEM((pieces, SLOTS, WIDE), F32),
            pltpu.VMEM((pieces, SLOTS, WIDE), BF16),
            pltpu.VMEM((NZ - 1, GROUPS, SLOTS, WIDE), BF16),
            pltpu.VMEM((GROUPS, SLOTS, WIDE), BF16),
            dma((1 + GROUPS, 6)), dma((1 + GROUPS, 6)), dma((1 + GROUPS, 2)),
            dma((3, 5)), dma((3, 5)), dma,
            dma((2, 7)), dma((OWN,)), dma((NZ,)),
            dma((GROUPS,)), dma((GROUPS,)),
            dma((2, 14)), dma((2, 14)),
            dma((pieces,)), dma((pieces,)),
            dma((pieces,)), dma((pieces,)),
            dma((pieces,)), dma,
        ],
        compiler_params=pltpu.CompilerParams(
            collective_id=0, has_side_effects=True, vmem_limit_bytes=60 * 2**20
        ),
    )(hist_len, cand_start, slot_cand, history[0], candidates[0], w_kv, w_qu, w_o)
    return out[None]


def solution(mesh):
    in_specs = (
        P("user", "seq", None),
        P("user"),
        P("user", None),
        P("user", "seq", None),
        P("user", "seq"),
        P("user", None),
        P("user", None),
        P("user", None),
    )
    out_specs = P("user", "seq", None)
    return jax.shard_map(local, mesh=mesh, in_specs=in_specs, out_specs=out_specs, check_vma=False)
```
